256 devices in a mesh: stn: 16 (over z_hi, x, core), tm: 16 (over z_lo, y).
Axes of the slice: x: 4, y: 4, z: 8 (z_hi: 2, z_lo: 4; z = z_hi * 4 + z_lo), core: 2. Of those that a mesh axis runs over, the one named last changes fastest.
Arguments:
- volts: bfloat16 [256, 1048576], P('stn', 'tm'), may hold values from -8 to 8
- taps: float32 [12, 2048], replicated, may hold values from -1.75 to 1.75
- tile_pairs: int32 [3, 2], replicated, may hold values from 0 to 1, as said below
Outputs:
- visibility: float32 [2, 1024, 3, 128, 128], P(None, ('stn', 'tm'))
The draws below stay inside these ranges and needn't reach their ends.
Inputs may be any that keep to these rules, and one draw needn't show every extreme that they name: `tile_pairs`: every pair (a, b) with a <= b < 2 appears exactly once, a first, in an order drawn from the seed.
All inputs are finite; a program needn't handle non-finite values.
Results may differ from the reference program's by a relative error of at most 0.0018.
Values may be sent and summed in bfloat16 or wider, within the bound.
No kernel may reach another device: no remote copies, remote signals or barrier semaphores. Data moves between devices by JAX's collectives and lax.ppermute only.
A program may use at most 128 MiB of HBM per device.

```python
import jax
import jax.numpy as jnp
from jax import lax

NIN = 256
NCH = 1024
FFT = 2048
TAPS = 12
TILE = 128
NTILE = 3
SPEC_DEV = 32
SPECTRA = 512
SAMPLES = 1048576
N_TM = 16


def draw_volts(key, part):
    key = jax.random.fold_in(key, 11)
    gain_key, noise_key = jax.random.split(key, 2)
    noise = jax.random.normal(noise_key, (NIN, SAMPLES), jnp.float32)
    gains = jnp.exp(jax.random.uniform(gain_key, (NIN, 1), jnp.float32, jnp.log(0.5), jnp.log(2.0)))
    values = gains * noise
    return jnp.clip(values, -8.0, 8.0).astype(jnp.bfloat16)


def draw_tile_pairs(key, part):
    key = jax.random.fold_in(key, 23)
    blocks = NIN // TILE
    listed = []
    for first in range(blocks):
        for second in range(first, blocks):
            listed.append([first, second])
    table = jnp.array(listed, jnp.int32)
    order = jax.random.permutation(key, table.shape[0])
    return table[order]


def gaussian(own_key, dims, spread, limit, kind=jnp.bfloat16):
    return jnp.clip(spread * jax.random.normal(own_key, dims, jnp.float32), -limit, limit).astype(kind)


def setup_inputs(seed: int = 0) -> dict:
    seeds = jax.random.split(jax.random.key(seed), 4)
    volts = draw_volts(jax.random.fold_in(seeds[3], 71), 0)
    taps = gaussian(seeds[1], (TAPS, FFT), TAPS ** -0.5, 1.75, jnp.float32)
    tile_pairs = draw_tile_pairs(jax.random.fold_in(seeds[3], 71), 0)
    return dict(volts=volts, taps=taps, tile_pairs=tile_pairs)


def tile_grams(stacked, tile_pairs):
    real_parts = []
    imag_parts = []
    for number in range(NTILE):
        left_rows = lax.dynamic_slice_in_dim(stacked, (tile_pairs[number, 0] * TILE).astype(jnp.int32), TILE, 0).astype(jnp.float32)
        right_rows = lax.dynamic_slice_in_dim(stacked, (tile_pairs[number, 1] * TILE).astype(jnp.int32), TILE, 0).astype(jnp.float32)
        real_parts.append(jnp.einsum('ispc,jspc->cij', left_rows, right_rows))
        imag_parts.append(jnp.einsum('isc,jsc->cij', left_rows[:, :, 1], right_rows[:, :, 0]) - jnp.einsum('isc,jsc->cij', left_rows[:, :, 0], right_rows[:, :, 1]))
    return jnp.stack([jnp.stack(real_parts, 1), jnp.stack(imag_parts, 1)], 0)

def reference(volts, taps, tile_pairs):
    frames = volts.reshape(NIN, SPECTRA, FFT)
    padded = jnp.concatenate([jnp.zeros((NIN, TAPS - 1, FFT), volts.dtype), frames], axis=1)

    def block_step(accum, index):
        start = (index * SPEC_DEV).astype(jnp.int32)
        window = lax.dynamic_slice_in_dim(padded, start, SPEC_DEV + TAPS - 1, 1)
        filtered = jnp.zeros((NIN, SPEC_DEV, FFT), jnp.float32)
        for step in range(TAPS):
            filtered = filtered + window[:, step:step + SPEC_DEV].astype(jnp.float32) * taps[step].astype(jnp.float32)
        transform = jnp.fft.rfft(filtered, axis=-1)[..., :NCH]
        scaled_re = (jnp.real(transform) / jnp.sqrt(jnp.float32(FFT))).astype(jnp.bfloat16)
        scaled_im = (jnp.imag(transform) / jnp.sqrt(jnp.float32(FFT))).astype(jnp.bfloat16)
        stacked = jnp.stack([scaled_re, scaled_im], axis=2)
        return (accum + tile_grams(stacked, tile_pairs), None)
    start_sum = jnp.zeros((2, NCH, NTILE, TILE, TILE), jnp.float32)
    total, unused = lax.scan(block_step, start_sum, jnp.arange(N_TM, dtype=jnp.int32))
    return total / jnp.float32(SPECTRA)
```

```python
import functools
import math

import jax
import jax.numpy as jnp
import ml_dtypes
import numpy as np
from jax import lax
from jax.experimental import pallas as pl
from jax.experimental.pallas import tpu as pltpu
from jax.sharding import PartitionSpec as P

TILE = 128
LANES = 128
RADIX = 16
BACK = 5
BLOCK = 2
HALF = 16
VMEM_LIMIT = 48 * 1024 * 1024


def second_step_table(fft_len):
    length = fft_len // RADIX
    quarter = length // 2
    place = np.arange(length, dtype=np.int64)
    out = np.zeros((RADIX // 2, 2 * length, 2 * length), np.float64)

    def rows(kappa):
        chan = kappa + RADIX * np.arange(quarter, dtype=np.int64)
        angle = 2.0 * np.pi * ((chan[:, None] * place[None, :]) % fft_len) / fft_len
        return np.cos(angle), np.sin(angle)

    for pair in range(RADIX // 2):
        for slot in range(2):
            if pair == 0:
                kappa = 0 if slot == 0 else RADIX // 2
            else:
                kappa = pair if slot == 0 else RADIX - pair
            cos, sin = rows(kappa)
            first = slot * length
            if pair == 0:
                cols = slice(slot * length, (slot + 1) * length)
                out[pair, first : first + quarter, cols] = cos
                out[pair, first + quarter : first + length, cols] = -sin
            else:
                sign = 1.0 if slot == 0 else -1.0
                out[pair, first : first + quarter, :length] = cos
                out[pair, first : first + quarter, length:] = -sign * sin
                out[pair, first + quarter : first + length, :length] = -sin
                out[pair, first + quarter : first + length, length:] = -sign * cos
    out = (out / math.sqrt(fft_len)).astype(np.float32)
    high = out.astype(ml_dtypes.bfloat16)
    low = (out - high.astype(np.float32)).astype(ml_dtypes.bfloat16)
    return np.concatenate([high, low], axis=1)


def first_step(x):
    c1, c2, c3 = (math.cos(math.pi * j / 8) for j in (1, 2, 3))
    a = [x[n] + x[n + 8] for n in range(8)]
    b = [x[n] - x[n + 8] for n in range(8)]
    d = [None] + [b[n] - b[8 - n] for n in (1, 2, 3)]
    s = [None] + [b[n] + b[8 - n] for n in (1, 2, 3)]
    u, v = b[0] + c2 * d[2], b[0] - c2 * d[2]
    p, q = c1 * d[1] + c3 * d[3], c3 * d[1] - c1 * d[3]
    g, h = b[4] + c2 * s[2], b[4] - c2 * s[2]
    m, n = c3 * s[1] + c1 * s[3], c1 * s[1] - c3 * s[3]
    e = [a[n_] + a[n_ + 4] for n_ in range(4)]
    f = [a[n_] - a[n_ + 4] for n_ in range(4)]
    w, z = c2 * (f[1] - f[3]), c2 * (f[1] + f[3])
    even, odd = e[0] + e[2], e[1] + e[3]
    return [
        (even + odd, even - odd),
        (u + p, g + m),
        (f[0] + w, f[2] + z),
        (v + q, n - h),
        (e[0] - e[2], e[1] - e[3]),
        (v - q, h + n),
        (f[0] - w, z - f[2]),
        (u - p, m - g),
    ]


def spectra_kernel(plan, fft_len, keep_ref, *refs):
    source_count = 1 + max(src for taps in plan for src, _, _ in taps)
    sources = refs[:source_count]
    taps_ref, table_ref = refs[source_count : source_count + 2]
    out_ref, filt, high, low, turned = refs[-5:]
    rows = sources[0].shape[0]
    outputs = len(plan)
    tap_count = taps_ref.shape[0]
    keep = keep_ref[0] != 0

    @pl.loop(0, RADIX)
    def _(col):
        base = pl.multiple_of(col * LANES, LANES)
        weights = [
            jnp.broadcast_to(taps_ref[pl.ds(j, 1), pl.ds(base, LANES)], (rows, LANES)) for j in range(tap_count)
        ]
        for block in range(0, outputs, BLOCK):
            held = {}
            for out in range(block, block + BLOCK):
                sums = {False: None, True: None}
                for j, (src, frame, wiped) in enumerate(plan[out]):
                    if (src, frame) not in held:
                        lane = pl.multiple_of(frame * fft_len + base, LANES)
                        held[src, frame] = sources[src][:, pl.ds(lane, LANES)].astype(jnp.float32)
                    term = held[src, frame] * weights[j]
                    sums[wiped] = term if sums[wiped] is None else sums[wiped] + term
                total = sums[False]
                if sums[True] is not None:
                    total = total + jnp.where(keep, sums[True], 0.0)
                filt[pl.ds(out * rows, rows), pl.ds(base, LANES)] = total

    @pl.loop(0, outputs)
    def _(out):
        at = pl.ds(pl.multiple_of(out * rows, rows), rows)
        parts = first_step([filt[at, n * LANES : (n + 1) * LANES] for n in range(RADIX)])
        for pair, halves in enumerate(parts):
            for k, value in enumerate(halves):
                top = value.astype(jnp.bfloat16)
                high[pair, at, k * LANES : (k + 1) * LANES] = top
                low[pair, at, k * LANES : (k + 1) * LANES] = (value - top.astype(jnp.float32)).astype(jnp.bfloat16)

    quarter = fft_len // RADIX // 2
    per_dev = 4
    spread = RADIX // per_dev * 2 * per_dev

    def product(left, right):
        return lax.dot_general(left, right, (((1,), (1,)), ((), ())), preferred_element_type=jnp.float32)

    size = 2 * LANES
    for pair in range(RADIX // 2):
        table_high, table_low = table_ref[pair, :size], table_ref[pair, size:]
        result = (
            product(table_high, low[pair]) + product(table_low, high[pair])
        ) + product(table_high, high[pair])
        for slot in range(2):
            kappa = (pair, RADIX - pair)[slot] if pair else (0, RADIX // 2)[slot]
            for part in range(2):
                first = slot * LANES + part * quarter
                row = (kappa // per_dev) * 2 * per_dev + (kappa % per_dev) * 2 + part
                for lane in range(result.shape[1] // LANES):
                    turned[lane, pl.ds(row, quarter, stride=spread), :] = result[
                        first : first + quarter, lane * LANES : (lane + 1) * LANES
                    ]
    for lane in range(turned.shape[0]):
        out_ref[:, lane * LANES : (lane + 1) * LANES] = turned[lane].astype(jnp.bfloat16)


def spectra_call(plan, sources, taps, table, keep, half, previous):
    rows = sources[0].shape[0]
    fft_len = taps.shape[1]
    cols = len(plan) * rows
    vmem = pl.BlockSpec(memory_space=pltpu.VMEM)
    operands = [keep, *sources, taps, table]
    in_specs = [pl.BlockSpec(memory_space=pltpu.SMEM)] + [vmem] * (len(operands) - 1)
    aliases = {}
    if previous is not None:
        aliases = {len(operands): 0}
        operands.append(previous)
        in_specs.append(pl.BlockSpec(memory_space=pl.ANY))
    return pl.pallas_call(
        functools.partial(spectra_kernel, plan, fft_len),
        grid=(1,),
        out_shape=jax.ShapeDtypeStruct((fft_len, 2 * cols), jnp.bfloat16),
        in_specs=in_specs,
        out_specs=pl.BlockSpec((fft_len, cols), lambda i: (0, half)),
        scratch_shapes=[
            pltpu.VMEM((cols, fft_len), jnp.float32),
            pltpu.VMEM((RADIX // 2, cols, 2 * LANES), jnp.bfloat16),
            pltpu.VMEM((RADIX // 2, cols, 2 * LANES), jnp.bfloat16),
            pltpu.VMEM((cols // LANES, fft_len, LANES), jnp.float32),
        ],
        input_output_aliases=aliases,
        compiler_params=pltpu.CompilerParams(vmem_limit_bytes=VMEM_LIMIT),
        cost_estimate=pl.CostEstimate(flops=10**9, bytes_accessed=6 * 2**20, transcendentals=0),
        name="spectra%d" % half,
    )(*operands)


def gram_kernel(scale, pairs_ref, got_ref, out_ref, wide, left, right):
    groups = wide.shape[0]
    stations = 16
    times = 16
    chans = out_ref.shape[1]
    per_src = 2 * chans
    inputs = LANES // 8
    for group in range(groups):
        wide[group] = got_ref[:, group * LANES : (group + 1) * LANES].astype(jnp.float32)

    @pl.loop(0, stations)
    def _(stn):
        at = pl.ds(pl.multiple_of(stn * inputs, inputs), inputs)
        first = pl.multiple_of(stn * times * per_src, times * per_src)
        for chan in range(chans):
            parts = [
                [wide[group, pl.ds(first + chan * 2 + part, times, stride=per_src), :] for group in range(groups)]
                for part in range(2)
            ]
            plain = jnp.concatenate(parts[0] + parts[1], 0).T.astype(jnp.bfloat16)
            turned = jnp.concatenate([-v for v in parts[1]] + parts[0], 0).T.astype(jnp.bfloat16)
            for t in range(LANES // inputs):
                cols = slice(t * LANES, (t + 1) * LANES)
                left[chan, at, cols] = plain[t * inputs : (t + 1) * inputs]
                right[chan, at, cols] = turned[t * inputs : (t + 1) * inputs]

    def product(a, b):
        return lax.dot_general(a, b, (((1,), (1,)), ((), ())), preferred_element_type=jnp.float32)

    for tile in range(pairs_ref.shape[0]):
        rows = pl.ds(pl.multiple_of(pairs_ref[tile, 0] * TILE, TILE), TILE)
        cols = pl.ds(pl.multiple_of(pairs_ref[tile, 1] * TILE, TILE), TILE)
        for chan in range(chans):
            one = left[chan, rows, :]
            out_ref[0, chan, tile] = product(one, left[chan, cols, :]) * scale
            out_ref[1, chan, tile] = product(one, right[chan, cols, :]) * scale


def gram_call(got, tile_pairs, chans, total_spectra):
    rows, lanes = got.shape
    stations = 256
    depth = 8 * LANES
    vmem = pl.BlockSpec(memory_space=pltpu.VMEM)
    return pl.pallas_call(
        functools.partial(gram_kernel, 1.0 / total_spectra),
        out_shape=jax.ShapeDtypeStruct((2, chans, tile_pairs.shape[0], TILE, TILE), jnp.float32),
        in_specs=[pl.BlockSpec(memory_space=pltpu.SMEM), vmem],
        out_specs=vmem,
        scratch_shapes=[
            pltpu.VMEM((lanes // LANES, rows, LANES), jnp.float32),
            pltpu.VMEM((chans, stations, depth), jnp.bfloat16),
            pltpu.VMEM((chans, stations, depth), jnp.bfloat16),
        ],
        compiler_params=pltpu.CompilerParams(vmem_limit_bytes=VMEM_LIMIT),
        name="grams",
    )(tile_pairs, got)


def plans(frames, tap_count):
    ahead = tap_count - 1 - BACK

    def tap(out, j):
        frame = out - (tap_count - 1) + j
        if frame < 0:
            return (1, frame + ahead, False)
        if frame >= frames:
            return (2, frame - frames, False)
        return (0, frame, out >= frames)

    def plan(outs):
        return tuple(tuple(tap(out, j) for j in range(tap_count)) for out in outs)

    middle = list(range(tap_count - 1, tap_count - 1 + HALF))
    rest = list(range(tap_count - 1 + HALF, frames + BACK)) + list(range(BACK, tap_count - 1))
    return plan(middle), plan(rest)


def shards(volts, taps, tile_pairs):
    tap_count, fft_len = taps.shape
    frames = volts.shape[1] // fft_len
    peers = lax.axis_size("tm")
    ahead = tap_count - 1 - BACK
    earlier = lax.ppermute(
        volts[:, (frames - ahead) * fft_len :], "tm", [(i, i + 1) for i in range(peers - 1)]
    )
    later = lax.ppermute(volts[:, : BACK * fft_len], "tm", [(i, (i - 1) % peers) for i in range(peers)])
    table = jnp.asarray(second_step_table(fft_len))
    middle, rest = plans(frames, tap_count)
    keep = (lax.axis_index("tm") != peers - 1).astype(jnp.int32).reshape(1)
    spectra = spectra_call(middle, [volts], taps, table, keep, 0, None)
    spectra = spectra_call(rest, [volts, earlier, later], taps, table, keep, 1, spectra)
    devices = peers * lax.axis_size("stn")
    chans = fft_len // 2 // devices
    blocks = spectra.reshape(devices, 2 * chans, spectra.shape[1])
    got = lax.all_to_all(blocks, ("stn", "tm"), split_axis=0, concat_axis=0, tiled=True)
    return gram_call(got.reshape(spectra.shape), tile_pairs, chans, frames * peers)


def solution(mesh):
    return jax.shard_map(
        shards,
        mesh=mesh,
        in_specs=(P("stn", "tm"), P(), P()),
        out_specs=P(None, ("stn", "tm"), None, None, None),
        check_vma=False,
    )
```

```python
import functools
import math

import jax
import jax.numpy as jnp
import ml_dtypes
import numpy as np
from jax import lax
from jax.experimental import pallas as pl
from jax.experimental.pallas import tpu as pltpu
from jax.sharding import PartitionSpec as P

TILE = 128
LANES = 128
RADIX = 16
BACK = 5
BLOCK = 2
HALF = 16
Z_HIGH, PLANE, Z_LOW, Y_SIZE = 2, 8, 4, 4
Z_LOW_ORDER = (0, 2, 1, 3)
VMEM_LIMIT = 48 * 1024 * 1024


def device_order():
    order = []
    for plane in range(PLANE):
        for y in range(Y_SIZE):
            for low in Z_LOW_ORDER:
                for high in range(Z_HIGH):
                    order.append(((high * PLANE + plane) * Z_LOW + low) * Y_SIZE + y)
    return order


def second_step_table(fft_len):
    length = fft_len // RADIX
    quarter = length // 2
    place = np.arange(length, dtype=np.int64)
    out = np.zeros((RADIX // 2, 2 * length, 2 * length), np.float64)
    column = np.array([dev // Y_SIZE for dev in device_order() if dev % Y_SIZE == 0], np.int64)

    def rows(kappa):
        chan = kappa + RADIX * column
        angle = 2.0 * np.pi * ((chan[:, None] * place[None, :]) % fft_len) / fft_len
        return np.cos(angle), np.sin(angle)

    for pair in range(RADIX // 2):
        for slot in range(2):
            if pair == 0:
                kappa = 0 if slot == 0 else RADIX // 2
            else:
                kappa = pair if slot == 0 else RADIX - pair
            cos, sin = rows(kappa)
            first = slot * length
            if pair == 0:
                cols = slice(slot * length, (slot + 1) * length)
                out[pair, first : first + quarter, cols] = cos
                out[pair, first + quarter : first + length, cols] = -sin
            else:
                sign = 1.0 if slot == 0 else -1.0
                out[pair, first : first + quarter, :length] = cos
                out[pair, first : first + quarter, length:] = -sign * sin
                out[pair, first + quarter : first + length, :length] = -sin
                out[pair, first + quarter : first + length, length:] = -sign * cos
    out = (out / math.sqrt(fft_len)).astype(np.float32)
    high = out.astype(ml_dtypes.bfloat16)
    low = (out - high.astype(np.float32)).astype(ml_dtypes.bfloat16)
    return np.concatenate([high, low], axis=1)


def first_step(x):
    c1, c2, c3 = (math.cos(math.pi * j / 8) for j in (1, 2, 3))
    a = [x[n] + x[n + 8] for n in range(8)]
    b = [x[n] - x[n + 8] for n in range(8)]
    d = [None] + [b[n] - b[8 - n] for n in (1, 2, 3)]
    s = [None] + [b[n] + b[8 - n] for n in (1, 2, 3)]
    u, v = b[0] + c2 * d[2], b[0] - c2 * d[2]
    p, q = c1 * d[1] + c3 * d[3], c3 * d[1] - c1 * d[3]
    g, h = b[4] + c2 * s[2], b[4] - c2 * s[2]
    m, n = c3 * s[1] + c1 * s[3], c1 * s[1] - c3 * s[3]
    e = [a[n_] + a[n_ + 4] for n_ in range(4)]
    f = [a[n_] - a[n_ + 4] for n_ in range(4)]
    w, z = c2 * (f[1] - f[3]), c2 * (f[1] + f[3])
    even, odd = e[0] + e[2], e[1] + e[3]
    return [
        (even + odd, even - odd),
        (u + p, g + m),
        (f[0] + w, f[2] + z),
        (v + q, n - h),
        (e[0] - e[2], e[1] - e[3]),
        (v - q, h + n),
        (f[0] - w, z - f[2]),
        (u - p, m - g),
    ]


def filter_outputs(plan, fft_len, keep, sources, taps_ref, filt, blocks=None):
    rows = sources[0].shape[0]
    tap_count = taps_ref.shape[0]

    @pl.loop(0, RADIX)
    def _(col):
        base = pl.multiple_of(col * LANES, LANES)
        weights = [
            jnp.broadcast_to(taps_ref[pl.ds(j, 1), pl.ds(base, LANES)], (rows, LANES)) for j in range(tap_count)
        ]
        for block in range(0, len(plan), BLOCK):
            held = {}
            for out in range(block, min(block + BLOCK, len(plan))):
                sums = {False: None, True: None}
                for j, (src, frame, wiped) in enumerate(plan[out]):
                    if (src, frame) not in held:
                        lane = pl.multiple_of(frame * fft_len + base, LANES)
                        held[src, frame] = sources[src][:, pl.ds(lane, LANES)].astype(jnp.float32)
                    term = held[src, frame] * weights[j]
                    sums[wiped] = term if sums[wiped] is None else sums[wiped] + term
                total = sums[False]
                if sums[True] is not None:
                    total = total + jnp.where(keep, sums[True], 0.0)
                filt[pl.ds(out * rows, rows), pl.ds(base, LANES)] = total


def first_steps(filt, rows, first, count, high, low, offset):
    @pl.loop(0, count)
    def _(out):
        at = pl.ds(pl.multiple_of((out + first) * rows, rows), rows)
        to = pl.ds(pl.multiple_of(out * rows + offset, rows), rows)
        parts = first_step([filt[at, n * LANES : (n + 1) * LANES] for n in range(RADIX)])
        for pair, halves in enumerate(parts):
            for k, value in enumerate(halves):
                top = value.astype(jnp.bfloat16)
                high[pair, to, k * LANES : (k + 1) * LANES] = top
                low[pair, to, k * LANES : (k + 1) * LANES] = (value - top.astype(jnp.float32)).astype(jnp.bfloat16)


def second_steps(table, high, low, turned, out_ref):
    quarter = PLANE * Z_HIGH * Z_LOW
    per_dev = 4
    z_size = Z_HIGH * Z_LOW
    block = 2 * per_dev

    def product(left, right):
        return lax.dot_general(left, right, (((1,), (1,)), ((), ())), preferred_element_type=jnp.float32)

    size = 2 * LANES
    for pair in range(RADIX // 2):
        table_high, table_low = table[pair, :size], table[pair, size:]
        result = (
            product(table_high, low[pair]) + product(table_low, high[pair])
        ) + product(table_high, high[pair])
        for slot in range(2):
            kappa = (pair, RADIX - pair)[slot] if pair else (0, RADIX // 2)[slot]
            for part in range(2):
                for plane in range(PLANE):
                    first = slot * LANES + part * quarter + plane * z_size
                    row = (plane * Y_SIZE + kappa // per_dev) * z_size * block + (kappa % per_dev) * 2 + part
                    for lane in range(result.shape[1] // LANES):
                        turned[lane, pl.ds(row, z_size, stride=block), :] = result[
                            first : first + z_size, lane * LANES : (lane + 1) * LANES
                        ]
    for lane in range(turned.shape[0]):
        out_ref[:, lane * LANES : (lane + 1) * LANES] = turned[lane].astype(jnp.bfloat16)


def middle_kernel(plan, fft_len, volts, taps, table_hbm, out_ref, more_high, more_low,
                  table, filt, high, low, turned, sems):
    rows = volts.shape[0]
    copy = pltpu.make_async_copy(table_hbm, table, sems.at[0])
    copy.start()
    filter_outputs(plan, fft_len, None, [volts], taps, filt)
    first_steps(filt, rows, 0, HALF, high, low, 0)
    first_steps(filt, rows, HALF, len(plan) - HALF, more_high, more_low, 0)
    copy.wait()
    second_steps(table, high, low, turned, out_ref)


def edge_kernel(plan, fft_len, keep_ref, volts, taps, table_hbm, earlier, later, more_high, more_low, _,
                out_ref, table, filt, high, low, turned, sems):
    rows = volts.shape[0]
    copies = [
        pltpu.make_async_copy(more_high, high.at[:, pl.ds(0, more_high.shape[1])], sems.at[0]),
        pltpu.make_async_copy(more_low, low.at[:, pl.ds(0, more_low.shape[1])], sems.at[1]),
        pltpu.make_async_copy(table_hbm, table, sems.at[2]),
    ]
    for copy in copies:
        copy.start()
    filter_outputs(plan, fft_len, keep_ref[0] != 0, [volts, earlier, later], taps, filt)
    first_steps(filt, rows, 0, len(plan), high, low, more_high.shape[1])
    for copy in copies:
        copy.wait()
    second_steps(table, high, low, turned, out_ref)


def spectra_scratch(volts, taps, table, outputs, copies):
    rows, fft_len = volts.shape[0], taps.shape[1]
    cols = HALF * rows
    return [
        pltpu.VMEM(table.shape, table.dtype),
        pltpu.VMEM((outputs * rows, fft_len), jnp.float32),
        pltpu.VMEM((RADIX // 2, cols, 2 * LANES), jnp.bfloat16),
        pltpu.VMEM((RADIX // 2, cols, 2 * LANES), jnp.bfloat16),
        pltpu.VMEM((cols // LANES, fft_len, LANES), jnp.float32),
        pltpu.SemaphoreType.DMA((copies,)),
    ]


def middle_call(plan, volts, taps, table):
    rows, fft_len = volts.shape[0], taps.shape[1]
    cols = HALF * rows
    more = jax.ShapeDtypeStruct((RADIX // 2, (len(plan) - HALF) * rows, 2 * LANES), jnp.bfloat16)
    whole = pl.BlockSpec(more.shape, lambda i: (0, 0, 0))
    vmem = pl.BlockSpec(memory_space=pltpu.VMEM)
    return pl.pallas_call(
        functools.partial(middle_kernel, plan, fft_len),
        grid=(1,),
        out_shape=(pltpu.HBM((fft_len, 2 * cols), jnp.bfloat16), more, more),
        in_specs=[vmem, vmem, pl.BlockSpec(memory_space=pl.ANY)],
        out_specs=(pl.BlockSpec((fft_len, cols), lambda i: (0, 0)), whole, whole),
        scratch_shapes=spectra_scratch(volts, taps, table, len(plan), 1),
        compiler_params=pltpu.CompilerParams(vmem_limit_bytes=VMEM_LIMIT),
        cost_estimate=pl.CostEstimate(flops=10**9, bytes_accessed=8 * 2**20, transcendentals=0),
        name="middle",
    )(volts, taps, table)


def edge_call(plan, keep, volts, taps, table, earlier, later, more_high, more_low, spectra):
    rows, fft_len = volts.shape[0], taps.shape[1]
    cols = HALF * rows
    hbm = pl.BlockSpec(memory_space=pl.ANY)
    vmem = pl.BlockSpec(memory_space=pltpu.VMEM)
    return pl.pallas_call(
        functools.partial(edge_kernel, plan, fft_len),
        grid=(1,),
        out_shape=pltpu.HBM(spectra.shape, spectra.dtype),
        in_specs=[pl.BlockSpec(memory_space=pltpu.SMEM), vmem, vmem, hbm, vmem, vmem, hbm, hbm, hbm],
        out_specs=pl.BlockSpec((fft_len, cols), lambda i: (0, 1)),
        scratch_shapes=spectra_scratch(volts, taps, table, len(plan), 3),
        input_output_aliases={8: 0},
        compiler_params=pltpu.CompilerParams(vmem_limit_bytes=VMEM_LIMIT),
        cost_estimate=pl.CostEstimate(flops=10**9, bytes_accessed=8 * 2**20, transcendentals=0),
        name="edge",
    )(keep, volts, taps, table, earlier, later, more_high, more_low, spectra)


def ends_kernel(volts, last_ref, first_ref, sems):
    size = last_ref.shape[1]
    copies = [
        pltpu.make_async_copy(volts.at[:, pl.ds(volts.shape[1] - size, size)], last_ref, sems.at[0]),
        pltpu.make_async_copy(volts.at[:, pl.ds(0, first_ref.shape[1])], first_ref, sems.at[1]),
    ]
    for copy in copies:
        copy.start()
    for copy in copies:
        copy.wait()


def ends_call(volts, last, first):
    vmem = pl.BlockSpec(memory_space=pltpu.VMEM)
    rows = volts.shape[0]
    return pl.pallas_call(
        ends_kernel,
        out_shape=(jax.ShapeDtypeStruct((rows, last), volts.dtype), jax.ShapeDtypeStruct((rows, first), volts.dtype)),
        in_specs=[pl.BlockSpec(memory_space=pl.ANY)],
        out_specs=(vmem, vmem),
        scratch_shapes=[pltpu.SemaphoreType.DMA((2,))],
        name="ends",
    )(volts)


def gram_kernel(scale, pairs_ref, got_ref, out_ref, wide, both, tiles):
    groups = wide.shape[0]
    per_src = 8
    times = Y_SIZE * Z_LOW
    inputs = LANES // 8
    pitch = 3 * per_src
    chan = pl.program_id(0)

    @pl.when(chan == 0)
    def _():
        @pl.loop(0, got_ref.shape[0] // (2 * per_src), unroll=8)
        def _(two):
            from_rows = pl.ds(pl.multiple_of(two * 2 * per_src, 2 * per_src), 2 * per_src)
            to_rows = pl.ds(pl.multiple_of(two * pitch, per_src), 2 * per_src)
            for group in range(groups):
                wide[group, to_rows] = got_ref[from_rows, group * LANES : (group + 1) * LANES].astype(jnp.float32)

    stations = Z_HIGH * PLANE * inputs

    @pl.loop(0, Z_HIGH * PLANE, unroll=16)
    def _(stn):
        at = pl.ds(pl.multiple_of(stn * inputs, inputs), inputs)
        turned_at = pl.ds(pl.multiple_of(stations + stn * inputs, inputs), inputs)
        first = (stn % PLANE) * times * pitch + (stn // PLANE) * per_src + chan * 2
        parts = [
            [wide[group, pl.ds(first + part, times, stride=pitch), :] for group in range(groups)] for part in range(2)
        ]
        plain = jnp.concatenate(parts[0] + parts[1], 0).astype(jnp.bfloat16).T
        turned = jnp.concatenate([-v for v in parts[1]] + parts[0], 0).astype(jnp.bfloat16).T
        for t in range(LANES // inputs):
            cols = slice(t * LANES, (t + 1) * LANES)
            both[at, cols] = plain[t * inputs : (t + 1) * inputs]
            both[turned_at, cols] = turned[t * inputs : (t + 1) * inputs]

    sums = lax.dot_general(
        both[:stations], both[...], (((1,), (1,)), ((), ())), preferred_element_type=jnp.float32
    )
    for first in range(2):
        for second in range(2):
            for part in range(2):
                col = part * stations + second * TILE
                tiles[first, second, part] = sums[first * TILE : (first + 1) * TILE, col : col + TILE] * scale
    for tile in range(pairs_ref.shape[0]):
        for part in range(2):
            out_ref[part, 0, tile] = tiles[pairs_ref[tile, 0], pairs_ref[tile, 1], part]


def gram_call(got, tile_pairs, chans, total_spectra):
    rows, lanes = got.shape
    stations = 2 * TILE
    depth = 8 * LANES
    tiles = tile_pairs.shape[0]
    return pl.pallas_call(
        functools.partial(gram_kernel, 1.0 / total_spectra),
        grid=(chans,),
        out_shape=jax.ShapeDtypeStruct((2, chans, tiles, TILE, TILE), jnp.float32),
        in_specs=[pl.BlockSpec(memory_space=pltpu.SMEM), pl.BlockSpec(memory_space=pltpu.VMEM)],
        out_specs=pl.BlockSpec((2, 1, tiles, TILE, TILE), lambda i: (0, i, 0, 0, 0)),
        scratch_shapes=[
            pltpu.VMEM((lanes // LANES, rows // 2 * 3, LANES), jnp.float32),
            pltpu.VMEM((2 * stations, depth), jnp.bfloat16),
            pltpu.VMEM((2, 2, 2, TILE, TILE), jnp.float32),
        ],
        compiler_params=pltpu.CompilerParams(vmem_limit_bytes=VMEM_LIMIT),
        name="grams",
    )(tile_pairs, got)


def plans(frames, tap_count):
    ahead = tap_count - 1 - BACK

    def tap(out, j):
        frame = out - (tap_count - 1) + j
        if frame < 0:
            return (1, frame + ahead, False)
        if frame >= frames:
            return (2, frame - frames, False)
        return (0, frame, out >= frames)

    def plan(outs):
        return tuple(tuple(tap(out, j) for j in range(tap_count)) for out in outs)

    middle = list(range(tap_count - 1, frames))
    edges = list(range(BACK, tap_count - 1)) + list(range(frames, frames + BACK))
    return plan(middle), plan(edges)


def shards(volts, taps, tile_pairs):
    tap_count, fft_len = taps.shape
    frames = volts.shape[1] // fft_len
    peers = lax.axis_size("tm")
    last, first = ends_call(volts, (tap_count - 1 - BACK) * fft_len, BACK * fft_len)
    earlier = lax.ppermute(last, "tm", [(i, i + 1) for i in range(peers - 1)])
    later = lax.ppermute(first, "tm", [(i, (i - 1) % peers) for i in range(peers)])
    table = jnp.asarray(second_step_table(fft_len))
    middle, edges = plans(frames, tap_count)
    keep = (lax.axis_index("tm") != peers - 1).astype(jnp.int32).reshape(1)
    spectra, more_high, more_low = middle_call(middle, volts, taps, table)
    spectra = edge_call(edges, keep, volts, taps, table, earlier, later, more_high, more_low, spectra)
    order = device_order()
    chans = fft_len // 2 // len(order)
    blocks = spectra.reshape(len(order), 2 * chans, spectra.shape[1])
    got = lax.all_to_all(
        blocks, ("stn", "tm"), split_axis=0, concat_axis=0, tiled=True, axis_index_groups=[order]
    )
    return gram_call(got.reshape(spectra.shape), tile_pairs, chans, frames * peers)


def solution(mesh):
    return jax.shard_map(
        shards,
        mesh=mesh,
        in_specs=(P("stn", "tm"), P(), P()),
        out_specs=P(None, ("stn", "tm"), None, None, None),
        check_vma=False,
    )
```

```python
import functools
import math

import jax
import jax.numpy as jnp
import ml_dtypes
import numpy as np
from jax import lax
from jax.experimental import pallas as pl
from jax.experimental.pallas import tpu as pltpu
from jax.sharding import PartitionSpec as P

TILE = 128
LANES = 128
RADIX = 16
BACK = 5
BLOCK = 2
HALF = 16
Z_HIGH, PLANE, Z_LOW, Y_SIZE = 2, 8, 4, 4
Z_LOW_ORDER = (0, 2, 1, 3)
VMEM_LIMIT = 48 * 1024 * 1024


def device_order():
    order = []
    for plane in range(PLANE):
        for y in range(Y_SIZE):
            for low in Z_LOW_ORDER:
                for high in range(Z_HIGH):
                    order.append(((high * PLANE + plane) * Z_LOW + low) * Y_SIZE + y)
    return order


def second_step_table(fft_len):
    length = fft_len // RADIX
    quarter = length // 2
    place = np.arange(length, dtype=np.int64)
    out = np.zeros((RADIX // 2, 2 * length, 2 * length), np.float64)
    column = np.array([dev // Y_SIZE for dev in device_order() if dev % Y_SIZE == 0], np.int64)

    def rows(kappa):
        chan = kappa + RADIX * column
        angle = 2.0 * np.pi * ((chan[:, None] * place[None, :]) % fft_len) / fft_len
        return np.cos(angle), np.sin(angle)

    for pair in range(RADIX // 2):
        for slot in range(2):
            if pair == 0:
                kappa = 0 if slot == 0 else RADIX // 2
            else:
                kappa = pair if slot == 0 else RADIX - pair
            cos, sin = rows(kappa)
            first = slot * length
            if pair == 0:
                cols = slice(slot * length, (slot + 1) * length)
                out[pair, first : first + quarter, cols] = cos
                out[pair, first + quarter : first + length, cols] = -sin
            else:
                sign = 1.0 if slot == 0 else -1.0
                out[pair, first : first + quarter, :length] = cos
                out[pair, first : first + quarter, length:] = -sign * sin
                out[pair, first + quarter : first + length, :length] = -sin
                out[pair, first + quarter : first + length, length:] = -sign * cos
    out = (out / math.sqrt(fft_len)).astype(np.float32)
    high = out.astype(ml_dtypes.bfloat16)
    low = (out - high.astype(np.float32)).astype(ml_dtypes.bfloat16)
    return np.concatenate([high, low], axis=1)


def first_step(x):
    c1, c2, c3 = (math.cos(math.pi * j / 8) for j in (1, 2, 3))
    a = [x[n] + x[n + 8] for n in range(8)]
    b = [x[n] - x[n + 8] for n in range(8)]
    d = [None] + [b[n] - b[8 - n] for n in (1, 2, 3)]
    s = [None] + [b[n] + b[8 - n] for n in (1, 2, 3)]
    u, v = b[0] + c2 * d[2], b[0] - c2 * d[2]
    p, q = c1 * d[1] + c3 * d[3], c3 * d[1] - c1 * d[3]
    g, h = b[4] + c2 * s[2], b[4] - c2 * s[2]
    m, n = c3 * s[1] + c1 * s[3], c1 * s[1] - c3 * s[3]
    e = [a[n_] + a[n_ + 4] for n_ in range(4)]
    f = [a[n_] - a[n_ + 4] for n_ in range(4)]
    w, z = c2 * (f[1] - f[3]), c2 * (f[1] + f[3])
    even, odd = e[0] + e[2], e[1] + e[3]
    return [
        (even + odd, even - odd),
        (u + p, g + m),
        (f[0] + w, f[2] + z),
        (v + q, n - h),
        (e[0] - e[2], e[1] - e[3]),
        (v - q, h + n),
        (f[0] - w, z - f[2]),
        (u - p, m - g),
    ]


def filter_outputs(plan, fft_len, keep, sources, taps_ref, base_ref, out_ref, start):
    rows = sources[0].shape[0]

    @pl.loop(0, RADIX)
    def _(col):
        base = pl.multiple_of(col * LANES, LANES)
        lanes = pl.ds(base, LANES)
        weights = [jnp.broadcast_to(taps_ref[pl.ds(j, 1), lanes], (rows, LANES)) for j in range(taps_ref.shape[0])]
        for block in range(0, len(plan), BLOCK):
            held = {}
            for out in range(block, min(block + BLOCK, len(plan))):
                at = pl.ds((start + out) * rows, rows)
                sums = {False: None if base_ref is None else base_ref[at, lanes], True: None}
                for j, src, frame, wiped in plan[out]:
                    if (src, frame) not in held:
                        lane = pl.multiple_of(frame * fft_len + base, LANES)
                        held[src, frame] = sources[src][:, pl.ds(lane, LANES)].astype(jnp.float32)
                    term = held[src, frame] * weights[j]
                    sums[wiped] = term if sums[wiped] is None else sums[wiped] + term
                total = sums[False]
                if sums[True] is not None:
                    wiped_sum = jnp.where(keep, sums[True], 0.0)
                    total = wiped_sum if total is None else total + wiped_sum
                out_ref[at, lanes] = total


def first_steps(filt, rows, first, count, high, low, offset):
    @pl.loop(0, count)
    def _(out):
        at = pl.ds(pl.multiple_of((out + first) * rows, rows), rows)
        to = pl.ds(pl.multiple_of(out * rows + offset, rows), rows)
        parts = first_step([filt[at, n * LANES : (n + 1) * LANES] for n in range(RADIX)])
        for pair, halves in enumerate(parts):
            for k, value in enumerate(halves):
                top = value.astype(jnp.bfloat16)
                high[pair, to, k * LANES : (k + 1) * LANES] = top
                low[pair, to, k * LANES : (k + 1) * LANES] = (value - top.astype(jnp.float32)).astype(jnp.bfloat16)


def second_steps(table, high, low, turned, ready, out_ref, half, sems):
    quarter = PLANE * Z_HIGH * Z_LOW
    per_dev = 4
    z_size = Z_HIGH * Z_LOW
    block = 2 * per_dev
    share = z_size * block
    cols = ready.shape[1]

    def product(left, right):
        return lax.dot_general(left, right, (((1,), (1,)), ((), ())), preferred_element_type=jnp.float32)

    def send(first_y, count, sem):
        copies = []
        for plane in range(PLANE):
            at = pl.ds((plane * Y_SIZE + first_y) * share, count * share)
            for lane in range(cols // LANES):
                ready[at, lane * LANES : (lane + 1) * LANES] = turned[lane, at].astype(jnp.bfloat16)
            copies.append(
                pltpu.make_async_copy(ready.at[at], out_ref.at[at, pl.ds(half * cols, cols)], sems.at[sem + plane])
            )
            copies[-1].start()
        return copies

    size = 2 * LANES
    copies = []
    for pair in range(RADIX // 2):
        table_high, table_low = table[pair, :size], table[pair, size:]
        result = (
            product(table_high, low[pair]) + product(table_low, high[pair])
        ) + product(table_high, high[pair])
        for slot in range(2):
            kappa = (pair, RADIX - pair)[slot] if pair else (0, RADIX // 2)[slot]
            for part in range(2):
                for plane in range(PLANE):
                    first = slot * LANES + part * quarter + plane * z_size
                    row = (plane * Y_SIZE + kappa // per_dev) * share + (kappa % per_dev) * 2 + part
                    for lane in range(cols // LANES):
                        turned[lane, pl.ds(row, z_size, stride=block), :] = result[
                            first : first + z_size, lane * LANES : (lane + 1) * LANES
                        ]
        if pair == 4:
            copies += send(0, 1, 0) + send(3, 1, PLANE)
    copies += send(1, 2, 2 * PLANE)
    for copy in copies:
        copy.wait()


def middle_kernel(plan, own, fft_len, keep_ref, volts_hbm, taps_hbm, table_hbm, out_ref, more_high, more_low, partial,
                  volts, taps, table, filt, high, low, turned, ready, out_sems, sems):
    rows = volts.shape[0]
    keep = keep_ref[0] != 0
    frames = volts.shape[1] // fft_len
    copies = [pltpu.make_async_copy(taps_hbm, taps, sems.at[0])]
    bounds = (0, 15, 21, 27, frames)
    for piece in range(4):
        part = pl.ds(bounds[piece] * fft_len, (bounds[piece + 1] - bounds[piece]) * fft_len)
        copies.append(pltpu.make_async_copy(volts_hbm.at[:, part], volts.at[:, part], sems.at[1 + piece]))
    copies.append(pltpu.make_async_copy(table_hbm, table, sems.at[5]))
    for copy in copies:
        copy.start()
    copies[0].wait()
    done = 0
    for piece in range(4):
        copies[1 + piece].wait()
        upto = bounds[piece + 1] - (taps.shape[0] - 1)
        filter_outputs(plan[done:upto], fft_len, keep, [volts], taps, None, filt, done)
        done = upto
    filter_outputs(own, fft_len, keep, [volts], taps, None, partial, 0)
    first_steps(filt, rows, 0, HALF, high, low, 0)
    first_steps(filt, rows, HALF, len(plan) - HALF, more_high, more_low, 0)
    copies[5].wait()
    second_steps(table, high, low, turned, ready, out_ref, 0, out_sems)


def edge_kernel(plan, fft_len, taps_hbm, table_hbm, earlier, later, partial, more_high, more_low, _, out_ref,
                taps, table, filt, high, low, turned, ready, out_sems, sems):
    rows = earlier.shape[0]
    copies = [
        pltpu.make_async_copy(more_high, high.at[:, pl.ds(0, more_high.shape[1])], sems.at[0]),
        pltpu.make_async_copy(more_low, low.at[:, pl.ds(0, more_low.shape[1])], sems.at[1]),
        pltpu.make_async_copy(table_hbm, table, sems.at[2]),
    ]
    first = pltpu.make_async_copy(taps_hbm, taps, sems.at[3])
    first.start()
    for copy in copies:
        copy.start()
    first.wait()
    filter_outputs(plan, fft_len, None, [earlier, later], taps, partial, filt, 0)
    first_steps(filt, rows, 0, len(plan), high, low, more_high.shape[1])
    for copy in copies:
        copy.wait()
    second_steps(table, high, low, turned, ready, out_ref, 1, out_sems)


def spectra_scratch(rows, fft_len, table, outputs):
    cols = HALF * rows
    return [
        pltpu.VMEM(table.shape, table.dtype),
        pltpu.VMEM((outputs * rows, fft_len), jnp.float32),
        pltpu.VMEM((RADIX // 2, cols, 2 * LANES), jnp.bfloat16),
        pltpu.VMEM((RADIX // 2, cols, 2 * LANES), jnp.bfloat16),
        pltpu.VMEM((cols // LANES, fft_len, LANES), jnp.float32),
        pltpu.VMEM((fft_len, cols), jnp.bfloat16),
        pltpu.SemaphoreType.DMA((3 * PLANE,)),
    ]


def middle_call(plan, own, keep, volts, taps, table):
    rows, fft_len = volts.shape[0], taps.shape[1]
    cols = HALF * rows
    more = jax.ShapeDtypeStruct((RADIX // 2, (len(plan) - HALF) * rows, 2 * LANES), jnp.bfloat16)
    partial = jax.ShapeDtypeStruct((len(own) * rows, fft_len), jnp.float32)
    hbm = pl.BlockSpec(memory_space=pltpu.HBM)
    vmem = pl.BlockSpec(memory_space=pltpu.VMEM)
    return pl.pallas_call(
        functools.partial(middle_kernel, plan, own, fft_len),
        out_shape=(pltpu.HBM((fft_len, 2 * cols), jnp.bfloat16), more, more, partial),
        in_specs=[pl.BlockSpec(memory_space=pltpu.SMEM), hbm, hbm, hbm],
        out_specs=(hbm, vmem, vmem, vmem),
        scratch_shapes=[pltpu.VMEM(volts.shape, volts.dtype), pltpu.VMEM(taps.shape, taps.dtype)]
        + spectra_scratch(rows, fft_len, table, len(plan))
        + [pltpu.SemaphoreType.DMA((6,))],
        compiler_params=pltpu.CompilerParams(vmem_limit_bytes=VMEM_LIMIT),
        cost_estimate=pl.CostEstimate(flops=10**9, bytes_accessed=8 * 2**20, transcendentals=0),
        name="middle",
    )(keep, *(pltpu.with_memory_space_constraint(x, pltpu.HBM) for x in (volts, taps, table)))


def edge_call(plan, taps, table, earlier, later, partial, more_high, more_low, spectra):
    rows, fft_len = earlier.shape[0], taps.shape[1]
    hbm = pl.BlockSpec(memory_space=pltpu.HBM)
    vmem = pl.BlockSpec(memory_space=pltpu.VMEM)
    anywhere = pl.BlockSpec(memory_space=pl.ANY)
    return pl.pallas_call(
        functools.partial(edge_kernel, plan, fft_len),
        out_shape=pltpu.HBM(spectra.shape, spectra.dtype),
        in_specs=[anywhere, anywhere, vmem, vmem, vmem, anywhere, anywhere, hbm],
        out_specs=hbm,
        scratch_shapes=[pltpu.VMEM(taps.shape, taps.dtype)]
        + spectra_scratch(rows, fft_len, table, len(plan))
        + [pltpu.SemaphoreType.DMA((4,))],
        input_output_aliases={7: 0},
        compiler_params=pltpu.CompilerParams(vmem_limit_bytes=VMEM_LIMIT),
        cost_estimate=pl.CostEstimate(flops=10**9, bytes_accessed=8 * 2**20, transcendentals=0),
        name="edge",
    )(
        taps, table, earlier, later, partial, more_high, more_low, spectra,
    )


def ends_kernel(volts, last_ref, first_ref, sems):
    size = last_ref.shape[1]
    copies = [
        pltpu.make_async_copy(volts.at[:, pl.ds(volts.shape[1] - size, size)], last_ref, sems.at[0]),
        pltpu.make_async_copy(volts.at[:, pl.ds(0, first_ref.shape[1])], first_ref, sems.at[1]),
    ]
    for copy in copies:
        copy.start()
    for copy in copies:
        copy.wait()


def ends_call(volts, last, first):
    vmem = pl.BlockSpec(memory_space=pltpu.VMEM)
    rows = volts.shape[0]
    return pl.pallas_call(
        ends_kernel,
        out_shape=(pltpu.VMEM((rows, last), volts.dtype), pltpu.VMEM((rows, first), volts.dtype)),
        in_specs=[pl.BlockSpec(memory_space=pltpu.HBM)],
        out_specs=(vmem, vmem),
        scratch_shapes=[pltpu.SemaphoreType.DMA((2,))],
        name="ends",
    )(pltpu.with_memory_space_constraint(volts, pltpu.HBM))


def gram_kernel(scale, pairs_ref, got_ref, out_ref, wide, both, tiles, sems):
    groups = wide.shape[0]
    per_src = 8
    times = Y_SIZE * Z_LOW
    inputs = LANES // 8
    pitch = 3 * per_src
    stations = Z_HIGH * PLANE * inputs

    @pl.loop(0, got_ref.shape[0] // (2 * per_src), unroll=8)
    def _(two):
        from_rows = pl.ds(pl.multiple_of(two * 2 * per_src, 2 * per_src), 2 * per_src)
        to_rows = pl.ds(pl.multiple_of(two * pitch, per_src), 2 * per_src)
        for group in range(groups):
            wide[group, to_rows] = got_ref[from_rows, group * LANES : (group + 1) * LANES].astype(jnp.float32)

    copies = []
    for chan in range(out_ref.shape[1]):
        for stn in range(Z_HIGH * PLANE):
            at = pl.ds(stn * inputs, inputs)
            turned_at = pl.ds(stations + stn * inputs, inputs)
            first = (stn % PLANE) * times * pitch + (stn // PLANE) * per_src + chan * 2
            parts = [
                [wide[group, pl.ds(first + part, times, stride=pitch), :] for group in range(groups)] for part in range(2)
            ]
            plain = jnp.concatenate(parts[0] + parts[1], 0).astype(jnp.bfloat16).T
            turned = jnp.concatenate([-v for v in parts[1]] + parts[0], 0).astype(jnp.bfloat16).T
            for t in range(LANES // inputs):
                cols = slice(t * LANES, (t + 1) * LANES)
                both[chan, at, cols] = plain[t * inputs : (t + 1) * inputs]
                both[chan, turned_at, cols] = turned[t * inputs : (t + 1) * inputs]
        sums = lax.dot_general(
            both[chan, :stations], both[chan], (((1,), (1,)), ((), ())), preferred_element_type=jnp.float32
        )
        for first in range(2):
            for second in range(2):
                for part in range(2):
                    col = part * stations + second * TILE
                    tiles[chan, first, second, part] = sums[first * TILE : (first + 1) * TILE, col : col + TILE] * scale
        for tile in range(pairs_ref.shape[0]):
            for part in range(2):
                copies.append(
                    pltpu.make_async_copy(
                        tiles.at[chan, pairs_ref[tile, 0], pairs_ref[tile, 1], part],
                        out_ref.at[part, chan, tile],
                        sems.at[len(copies)],
                    )
                )
                copies[-1].start()
    for copy in copies:
        copy.wait()


def gram_call(got, tile_pairs, chans, total_spectra):
    rows, lanes = got.shape
    stations = 2 * TILE
    depth = 8 * LANES
    tiles = tile_pairs.shape[0]
    return pl.pallas_call(
        functools.partial(gram_kernel, 1.0 / total_spectra),
        out_shape=jax.ShapeDtypeStruct((2, chans, tiles, TILE, TILE), jnp.float32),
        in_specs=[pl.BlockSpec(memory_space=pltpu.SMEM), pl.BlockSpec(memory_space=pltpu.VMEM)],
        out_specs=pl.BlockSpec(memory_space=pl.ANY),
        scratch_shapes=[
            pltpu.VMEM((lanes // LANES, rows // 2 * 3, LANES), jnp.float32),
            pltpu.VMEM((chans, 2 * stations, depth), jnp.bfloat16),
            pltpu.VMEM((chans, 2, 2, 2, TILE, TILE), jnp.float32),
            pltpu.SemaphoreType.DMA((2 * chans * tiles,)),
        ],
        compiler_params=pltpu.CompilerParams(vmem_limit_bytes=VMEM_LIMIT),
        name="grams",
    )(tile_pairs, got)


def plans(frames, tap_count):
    ahead = tap_count - 1 - BACK

    def taps(out):
        own, others = [], []
        for j in range(tap_count):
            frame = out - (tap_count - 1) + j
            if frame < 0:
                others.append((j, 0, frame + ahead, False))
            elif frame >= frames:
                others.append((j, 1, frame - frames, False))
            else:
                own.append((j, 0, frame, out >= frames))
        return own, others

    middle = [taps(out)[0] for out in range(tap_count - 1, frames)]
    edges = [taps(out) for out in [*range(BACK, tap_count - 1), *range(frames, frames + BACK)]]
    return middle, [own for own, _ in edges], [others for _, others in edges]


def shards(volts, taps, tile_pairs):
    tap_count, fft_len = taps.shape
    frames = volts.shape[1] // fft_len
    peers = lax.axis_size("tm")
    last, first = ends_call(volts, (tap_count - 1 - BACK) * fft_len, BACK * fft_len)
    earlier = lax.ppermute(last, "tm", [(i, i + 1) for i in range(peers - 1)])
    later = lax.ppermute(first, "tm", [(i, (i - 1) % peers) for i in range(peers)])
    table = jnp.asarray(second_step_table(fft_len))
    middle, own, others = plans(frames, tap_count)
    keep = (lax.axis_index("tm") != peers - 1).astype(jnp.int32).reshape(1)
    spectra, more_high, more_low, partial = middle_call(middle, own, keep, volts, taps, table)
    spectra = edge_call(others, taps, table, earlier, later, partial, more_high, more_low, spectra)
    order = device_order()
    chans = fft_len // 2 // len(order)
    blocks = spectra.reshape(len(order), 2 * chans, spectra.shape[1])
    got = lax.all_to_all(
        blocks, ("stn", "tm"), split_axis=0, concat_axis=0, tiled=True, axis_index_groups=[order]
    )
    return gram_call(got.reshape(spectra.shape), tile_pairs, chans, frames * peers)


def solution(mesh):
    return jax.shard_map(
        shards,
        mesh=mesh,
        in_specs=(P("stn", "tm"), P(), P()),
        out_specs=P(None, ("stn", "tm"), None, None, None),
        check_vma=False,
    )
```

```python
import functools
import math

import jax
import jax.numpy as jnp
import ml_dtypes
import numpy as np
from jax import lax
from jax.experimental import pallas as pl
from jax.experimental.pallas import tpu as pltpu
from jax.sharding import PartitionSpec as P

TILE = 128
LANES = 128
RADIX = 16
BACK = 5
BLOCK = 2
HALF = 16
Z_HIGH, PLANE, Z_LOW, Y_SIZE = 2, 8, 4, 4
Z_LOW_ORDER = (0, 2, 1, 3)
VMEM_LIMIT = 48 * 1024 * 1024


def device_order():
    order = []
    for plane in range(PLANE):
        for y in range(Y_SIZE):
            for low in Z_LOW_ORDER:
                for high in range(Z_HIGH):
                    order.append(((high * PLANE + plane) * Z_LOW + low) * Y_SIZE + y)
    return order


def second_step_table(fft_len):
    length = fft_len // RADIX
    quarter = length // 2
    place = np.arange(length, dtype=np.int64)
    out = np.zeros((RADIX // 2, 2 * length, 2 * length), np.float64)
    column = np.array([dev // Y_SIZE for dev in device_order() if dev % Y_SIZE == 0], np.int64)

    def rows(kappa):
        chan = kappa + RADIX * column
        angle = 2.0 * np.pi * ((chan[:, None] * place[None, :]) % fft_len) / fft_len
        return np.cos(angle), np.sin(angle)

    for pair in range(RADIX // 2):
        for slot in range(2):
            if pair == 0:
                kappa = 0 if slot == 0 else RADIX // 2
            else:
                kappa = pair if slot == 0 else RADIX - pair
            cos, sin = rows(kappa)
            first = slot * length
            if pair == 0:
                cols = slice(slot * length, (slot + 1) * length)
                out[pair, first : first + quarter, cols] = cos
                out[pair, first + quarter : first + length, cols] = -sin
            else:
                sign = 1.0 if slot == 0 else -1.0
                out[pair, first : first + quarter, :length] = cos
                out[pair, first : first + quarter, length:] = -sign * sin
                out[pair, first + quarter : first + length, :length] = -sin
                out[pair, first + quarter : first + length, length:] = -sign * cos
    out = (out / math.sqrt(fft_len)).astype(np.float32)
    high = out.astype(ml_dtypes.bfloat16)
    low = (out - high.astype(np.float32)).astype(ml_dtypes.bfloat16)
    return np.concatenate([high, low], axis=1)


def first_step(x):
    c1, c2, c3 = (math.cos(math.pi * j / 8) for j in (1, 2, 3))
    a = [x[n] + x[n + 8] for n in range(8)]
    b = [x[n] - x[n + 8] for n in range(8)]
    d = [None] + [b[n] - b[8 - n] for n in (1, 2, 3)]
    s = [None] + [b[n] + b[8 - n] for n in (1, 2, 3)]
    u, v = b[0] + c2 * d[2], b[0] - c2 * d[2]
    p, q = c1 * d[1] + c3 * d[3], c3 * d[1] - c1 * d[3]
    g, h = b[4] + c2 * s[2], b[4] - c2 * s[2]
    m, n = c3 * s[1] + c1 * s[3], c1 * s[1] - c3 * s[3]
    e = [a[n_] + a[n_ + 4] for n_ in range(4)]
    f = [a[n_] - a[n_ + 4] for n_ in range(4)]
    w, z = c2 * (f[1] - f[3]), c2 * (f[1] + f[3])
    even, odd = e[0] + e[2], e[1] + e[3]
    return [
        (even + odd, even - odd),
        (u + p, g + m),
        (f[0] + w, f[2] + z),
        (v + q, n - h),
        (e[0] - e[2], e[1] - e[3]),
        (v - q, h + n),
        (f[0] - w, z - f[2]),
        (u - p, m - g),
    ]


def filter_outputs(plan, fft_len, keep, sources, taps_ref, base_ref, out_ref, start):
    rows = sources[0].shape[0]

    @pl.loop(0, RADIX)
    def _(col):
        base = pl.multiple_of(col * LANES, LANES)
        lanes = pl.ds(base, LANES)
        weights = [jnp.broadcast_to(taps_ref[pl.ds(j, 1), lanes], (rows, LANES)) for j in range(taps_ref.shape[0])]
        for block in range(0, len(plan), BLOCK):
            held = {}
            for out in range(block, min(block + BLOCK, len(plan))):
                at = pl.ds((start + out) * rows, rows)
                sums = {False: None if base_ref is None else base_ref[at, lanes], True: None}
                for j, src, frame, wiped in plan[out]:
                    if (src, frame) not in held:
                        lane = pl.multiple_of(frame * fft_len + base, LANES)
                        held[src, frame] = sources[src][:, pl.ds(lane, LANES)].astype(jnp.float32)
                    term = held[src, frame] * weights[j]
                    sums[wiped] = term if sums[wiped] is None else sums[wiped] + term
                total = sums[False]
                if sums[True] is not None:
                    wiped_sum = jnp.where(keep, sums[True], 0.0)
                    total = wiped_sum if total is None else total + wiped_sum
                out_ref[at, lanes] = total


def first_steps(filt, rows, first, count, high, low, offset):
    @pl.loop(0, count)
    def _(out):
        at = pl.ds(pl.multiple_of((out + first) * rows, rows), rows)
        to = pl.ds(pl.multiple_of(out * rows + offset, rows), rows)
        parts = first_step([filt[at, n * LANES : (n + 1) * LANES] for n in range(RADIX)])
        for pair, halves in enumerate(parts):
            for k, value in enumerate(halves):
                top = value.astype(jnp.bfloat16)
                high[pair, to, k * LANES : (k + 1) * LANES] = top
                low[pair, to, k * LANES : (k + 1) * LANES] = (value - top.astype(jnp.float32)).astype(jnp.bfloat16)


def second_steps(table, high, low, turned, ready, out_ref, half, sems):
    quarter = PLANE * Z_HIGH * Z_LOW
    per_dev = 4
    z_size = Z_HIGH * Z_LOW
    block = 2 * per_dev
    share = z_size * block
    cols = ready.shape[1]

    def product(left, right):
        return lax.dot_general(left, right, (((1,), (1,)), ((), ())), preferred_element_type=jnp.float32)

    def send(first_y, count, sem):
        copies = []
        for plane in range(PLANE):
            at = pl.ds((plane * Y_SIZE + first_y) * share, count * share)
            for lane in range(cols // LANES):
                ready[at, lane * LANES : (lane + 1) * LANES] = turned[lane, at].astype(jnp.bfloat16)
            copies.append(
                pltpu.make_async_copy(ready.at[at], out_ref.at[at, pl.ds(half * cols, cols)], sems.at[sem + plane])
            )
            copies[-1].start()
        return copies

    size = 2 * LANES
    copies = []
    for pair in range(RADIX // 2):
        table_high, table_low = table[pair, :size], table[pair, size:]
        result = (
            product(table_high, low[pair]) + product(table_low, high[pair])
        ) + product(table_high, high[pair])
        for slot in range(2):
            kappa = (pair, RADIX - pair)[slot] if pair else (0, RADIX // 2)[slot]
            for part in range(2):
                for plane in range(PLANE):
                    first = slot * LANES + part * quarter + plane * z_size
                    row = (plane * Y_SIZE + kappa // per_dev) * share + (kappa % per_dev) * 2 + part
                    for lane in range(cols // LANES):
                        turned[lane, pl.ds(row, z_size, stride=block), :] = result[
                            first : first + z_size, lane * LANES : (lane + 1) * LANES
                        ]
        if pair == 4:
            copies += send(0, 1, 0) + send(3, 1, PLANE)
    copies += send(1, 2, 2 * PLANE)
    for copy in copies:
        copy.wait()


def middle_kernel(plan, own, fft_len, keep_ref, volts_hbm, taps_hbm, table_hbm, out_ref, more_high, more_low, partial,
                  taps, table, volts, filt, high, low, turned, ready, out_sems, sems):
    rows = volts.shape[0]
    keep = keep_ref[0] != 0
    frames = volts.shape[1] // fft_len
    copies = [pltpu.make_async_copy(taps_hbm, taps, sems.at[0])]
    bounds = (0, 15, 21, 27, frames)
    for piece in range(4):
        part = pl.ds(bounds[piece] * fft_len, (bounds[piece + 1] - bounds[piece]) * fft_len)
        copies.append(pltpu.make_async_copy(volts_hbm.at[:, part], volts.at[:, part], sems.at[1 + piece]))
    copies.append(pltpu.make_async_copy(table_hbm, table, sems.at[5]))
    for copy in copies:
        copy.start()
    copies[0].wait()
    done = 0
    for piece in range(4):
        copies[1 + piece].wait()
        upto = bounds[piece + 1] - (taps.shape[0] - 1)
        filter_outputs(plan[done:upto], fft_len, keep, [volts], taps, None, filt, done)
        done = upto
    filter_outputs(own, fft_len, keep, [volts], taps, None, partial, 0)
    first_steps(filt, rows, 0, HALF, high, low, 0)
    first_steps(filt, rows, HALF, len(plan) - HALF, more_high, more_low, 0)
    copies[5].wait()
    second_steps(table, high, low, turned, ready, out_ref, 0, out_sems)


def edge_kernel(plan, fft_len, taps, table, earlier, later, partial, more_high, more_low, _, out_ref,
                filt, high, low, turned, ready, out_sems, sems):
    rows = earlier.shape[0]
    copies = [
        pltpu.make_async_copy(more_high, high.at[:, pl.ds(0, more_high.shape[1])], sems.at[0]),
        pltpu.make_async_copy(more_low, low.at[:, pl.ds(0, more_low.shape[1])], sems.at[1]),
    ]
    for copy in copies:
        copy.start()
    filter_outputs(plan, fft_len, None, [earlier, later], taps, partial, filt, 0)
    first_steps(filt, rows, 0, len(plan), high, low, more_high.shape[1])
    for copy in copies:
        copy.wait()
    second_steps(table, high, low, turned, ready, out_ref, 1, out_sems)


def spectra_scratch(rows, fft_len, outputs):
    cols = HALF * rows
    return [
        pltpu.VMEM((outputs * rows, fft_len), jnp.float32),
        pltpu.VMEM((RADIX // 2, cols, 2 * LANES), jnp.bfloat16),
        pltpu.VMEM((RADIX // 2, cols, 2 * LANES), jnp.bfloat16),
        pltpu.VMEM((cols // LANES, fft_len, LANES), jnp.float32),
        pltpu.VMEM((fft_len, cols), jnp.bfloat16),
        pltpu.SemaphoreType.DMA((3 * PLANE,)),
    ]


def middle_call(plan, own, keep, volts, taps, table):
    rows, fft_len = volts.shape[0], taps.shape[1]
    cols = HALF * rows
    more = jax.ShapeDtypeStruct((RADIX // 2, (len(plan) - HALF) * rows, 2 * LANES), jnp.bfloat16)
    partial = jax.ShapeDtypeStruct((len(own) * rows, fft_len), jnp.float32)
    hbm = pl.BlockSpec(memory_space=pltpu.HBM)
    vmem = pl.BlockSpec(memory_space=pltpu.VMEM)
    return pl.pallas_call(
        functools.partial(middle_kernel, plan, own, fft_len),
        out_shape=(
            pltpu.HBM((fft_len, 2 * cols), jnp.bfloat16),
            *(pltpu.VMEM(x.shape, x.dtype) for x in (more, more, partial, taps, table)),
        ),
        in_specs=[pl.BlockSpec(memory_space=pltpu.SMEM), hbm, hbm, hbm],
        out_specs=(hbm, vmem, vmem, vmem, vmem, vmem),
        scratch_shapes=[pltpu.VMEM(volts.shape, volts.dtype)]
        + spectra_scratch(rows, fft_len, len(plan))
        + [pltpu.SemaphoreType.DMA((6,))],
        compiler_params=pltpu.CompilerParams(vmem_limit_bytes=VMEM_LIMIT),
        cost_estimate=pl.CostEstimate(flops=10**9, bytes_accessed=8 * 2**20, transcendentals=0),
        name="middle",
    )(keep, *(pltpu.with_memory_space_constraint(x, pltpu.HBM) for x in (volts, taps, table)))


def edge_call(plan, taps, table, earlier, later, partial, more_high, more_low, spectra):
    rows, fft_len = earlier.shape[0], taps.shape[1]
    hbm = pl.BlockSpec(memory_space=pltpu.HBM)
    vmem = pl.BlockSpec(memory_space=pltpu.VMEM)
    anywhere = pl.BlockSpec(memory_space=pl.ANY)
    return pl.pallas_call(
        functools.partial(edge_kernel, plan, fft_len),
        out_shape=pltpu.HBM(spectra.shape, spectra.dtype),
        in_specs=[vmem, vmem, vmem, vmem, vmem, anywhere, anywhere, hbm],
        out_specs=hbm,
        scratch_shapes=spectra_scratch(rows, fft_len, len(plan)) + [pltpu.SemaphoreType.DMA((2,))],
        input_output_aliases={7: 0},
        compiler_params=pltpu.CompilerParams(vmem_limit_bytes=VMEM_LIMIT),
        cost_estimate=pl.CostEstimate(flops=10**9, bytes_accessed=8 * 2**20, transcendentals=0),
        name="edge",
    )(
        taps, table, earlier, later, partial, more_high, more_low, spectra,
    )


def ends_kernel(volts, last_ref, first_ref, sems):
    size = last_ref.shape[1]
    copies = [
        pltpu.make_async_copy(volts.at[:, pl.ds(volts.shape[1] - size, size)], last_ref, sems.at[0]),
        pltpu.make_async_copy(volts.at[:, pl.ds(0, first_ref.shape[1])], first_ref, sems.at[1]),
    ]
    for copy in copies:
        copy.start()
    for copy in copies:
        copy.wait()


def ends_call(volts, last, first):
    vmem = pl.BlockSpec(memory_space=pltpu.VMEM)
    rows = volts.shape[0]
    return pl.pallas_call(
        ends_kernel,
        out_shape=(pltpu.VMEM((rows, last), volts.dtype), pltpu.VMEM((rows, first), volts.dtype)),
        in_specs=[pl.BlockSpec(memory_space=pltpu.HBM)],
        out_specs=(vmem, vmem),
        scratch_shapes=[pltpu.SemaphoreType.DMA((2,))],
        name="ends",
    )(pltpu.with_memory_space_constraint(volts, pltpu.HBM))


def gram_kernel(scale, pairs_ref, got_ref, out_ref, wide, both, tiles, sems):
    groups = wide.shape[0]
    per_src = 8
    times = Y_SIZE * Z_LOW
    inputs = LANES // 8
    pitch = 3 * per_src
    stations = Z_HIGH * PLANE * inputs

    copies = []
    for chan in range(out_ref.shape[1]):
        for stn in range(Z_HIGH * PLANE):
            if chan == 0 and stn < PLANE:
                for two in range(stn * times, (stn + 1) * times):
                    from_rows = pl.ds(two * 2 * per_src, 2 * per_src)
                    for group in range(groups):
                        wide[group, pl.ds(two * pitch, 2 * per_src)] = got_ref[
                            from_rows, group * LANES : (group + 1) * LANES
                        ].astype(jnp.float32)
            at = pl.ds(stn * inputs, inputs)
            turned_at = pl.ds(stations + stn * inputs, inputs)
            first = (stn % PLANE) * times * pitch + (stn // PLANE) * per_src + chan * 2
            parts = [
                [wide[group, pl.ds(first + part, times, stride=pitch), :] for group in range(groups)] for part in range(2)
            ]
            plain = jnp.concatenate(parts[0] + parts[1], 0).astype(jnp.bfloat16).T
            turned = jnp.concatenate([-v for v in parts[1]] + parts[0], 0).astype(jnp.bfloat16).T
            for t in range(LANES // inputs):
                cols = slice(t * LANES, (t + 1) * LANES)
                both[chan, at, cols] = plain[t * inputs : (t + 1) * inputs]
                both[chan, turned_at, cols] = turned[t * inputs : (t + 1) * inputs]
        sums = lax.dot_general(
            both[chan, :stations], both[chan], (((1,), (1,)), ((), ())), preferred_element_type=jnp.float32
        )
        for first in range(2):
            for second in range(2):
                for part in range(2):
                    col = part * stations + second * TILE
                    tiles[chan, first, second, part] = sums[first * TILE : (first + 1) * TILE, col : col + TILE] * scale
        for tile in range(pairs_ref.shape[0]):
            for part in range(2):
                copies.append(
                    pltpu.make_async_copy(
                        tiles.at[chan, pairs_ref[tile, 0], pairs_ref[tile, 1], part],
                        out_ref.at[part, chan, tile],
                        sems.at[len(copies)],
                    )
                )
                copies[-1].start()
    for copy in copies:
        copy.wait()


def gram_call(got, tile_pairs, chans, total_spectra):
    rows, lanes = got.shape
    stations = 2 * TILE
    depth = 8 * LANES
    tiles = tile_pairs.shape[0]
    return pl.pallas_call(
        functools.partial(gram_kernel, 1.0 / total_spectra),
        out_shape=jax.ShapeDtypeStruct((2, chans, tiles, TILE, TILE), jnp.float32),
        in_specs=[pl.BlockSpec(memory_space=pltpu.SMEM), pl.BlockSpec(memory_space=pltpu.VMEM)],
        out_specs=pl.BlockSpec(memory_space=pl.ANY),
        scratch_shapes=[
            pltpu.VMEM((lanes // LANES, rows // 2 * 3, LANES), jnp.float32),
            pltpu.VMEM((chans, 2 * stations, depth), jnp.bfloat16),
            pltpu.VMEM((chans, 2, 2, 2, TILE, TILE), jnp.float32),
            pltpu.SemaphoreType.DMA((2 * chans * tiles,)),
        ],
        compiler_params=pltpu.CompilerParams(vmem_limit_bytes=VMEM_LIMIT),
        name="grams",
    )(tile_pairs, got)


def plans(frames, tap_count):
    ahead = tap_count - 1 - BACK

    def taps(out):
        own, others = [], []
        for j in range(tap_count):
            frame = out - (tap_count - 1) + j
            if frame < 0:
                others.append((j, 0, frame + ahead, False))
            elif frame >= frames:
                others.append((j, 1, frame - frames, False))
            else:
                own.append((j, 0, frame, out >= frames))
        return own, others

    middle = [taps(out)[0] for out in range(tap_count - 1, frames)]
    edges = [taps(out) for out in [*range(BACK, tap_count - 1), *range(frames, frames + BACK)]]
    return middle, [own for own, _ in edges], [others for _, others in edges]


def shards(volts, taps, tile_pairs):
    tap_count, fft_len = taps.shape
    frames = volts.shape[1] // fft_len
    peers = lax.axis_size("tm")
    last, first = ends_call(volts, (tap_count - 1 - BACK) * fft_len, BACK * fft_len)
    earlier = lax.ppermute(last, "tm", [(i, i + 1) for i in range(peers - 1)])
    later = lax.ppermute(first, "tm", [(i, (i - 1) % peers) for i in range(peers)])
    table = jnp.asarray(second_step_table(fft_len))
    middle, own, others = plans(frames, tap_count)
    keep = (lax.axis_index("tm") != peers - 1).astype(jnp.int32).reshape(1)
    spectra, more_high, more_low, partial, taps, table = middle_call(middle, own, keep, volts, taps, table)
    spectra = edge_call(others, taps, table, earlier, later, partial, more_high, more_low, spectra)
    order = device_order()
    chans = fft_len // 2 // len(order)
    blocks = spectra.reshape(len(order), 2 * chans, spectra.shape[1])
    got = lax.all_to_all(
        blocks, ("stn", "tm"), split_axis=0, concat_axis=0, tiled=True, axis_index_groups=[order]
    )
    return gram_call(got.reshape(spectra.shape), tile_pairs, chans, frames * peers)


def solution(mesh):
    return jax.shard_map(
        shards,
        mesh=mesh,
        in_specs=(P("stn", "tm"), P(), P()),
        out_specs=P(None, ("stn", "tm"), None, None, None),
        check_vma=False,
    )
```

```python
import functools
import math

import jax
import jax.numpy as jnp
import ml_dtypes
import numpy as np
from jax import lax
from jax.experimental import pallas as pl
from jax.experimental.pallas import tpu as pltpu
from jax.sharding import PartitionSpec as P

TILE = 128
LANES = 128
RADIX = 16
BACK = 5
BLOCK = 2
HALF = 16
Z_HIGH, PLANE, Z_LOW, Y_SIZE = 2, 8, 4, 4
Z_LOW_ORDER = (0, 2, 1, 3)
VMEM_LIMIT = 48 * 1024 * 1024


def device_order():
    order = []
    for plane in range(PLANE):
        for y in range(Y_SIZE):
            for low in Z_LOW_ORDER:
                for high in range(Z_HIGH):
                    order.append(((high * PLANE + plane) * Z_LOW + low) * Y_SIZE + y)
    return order


def second_step_table(fft_len):
    length = fft_len // RADIX
    quarter = length // 2
    place = np.arange(length, dtype=np.int64)
    out = np.zeros((RADIX // 2, 2 * length, 2 * length), np.float64)
    column = np.array([dev // Y_SIZE for dev in device_order() if dev % Y_SIZE == 0], np.int64)

    def rows(kappa):
        chan = kappa + RADIX * column
        angle = 2.0 * np.pi * ((chan[:, None] * place[None, :]) % fft_len) / fft_len
        return np.cos(angle), np.sin(angle)

    for pair in range(RADIX // 2):
        for slot in range(2):
            if pair == 0:
                kappa = 0 if slot == 0 else RADIX // 2
            else:
                kappa = pair if slot == 0 else RADIX - pair
            cos, sin = rows(kappa)
            first = slot * length
            if pair == 0:
                cols = slice(slot * length, (slot + 1) * length)
                out[pair, first : first + quarter, cols] = cos
                out[pair, first + quarter : first + length, cols] = -sin
            else:
                sign = 1.0 if slot == 0 else -1.0
                out[pair, first : first + quarter, :length] = cos
                out[pair, first : first + quarter, length:] = -sign * sin
                out[pair, first + quarter : first + length, :length] = -sin
                out[pair, first + quarter : first + length, length:] = -sign * cos
    out = (out / math.sqrt(fft_len)).astype(np.float32)
    high = out.astype(ml_dtypes.bfloat16)
    low = (out - high.astype(np.float32)).astype(ml_dtypes.bfloat16)
    return np.concatenate([high, low], axis=1)


def first_step(x):
    c1, c2, c3 = (math.cos(math.pi * j / 8) for j in (1, 2, 3))
    a = [x[n] + x[n + 8] for n in range(8)]
    b = [x[n] - x[n + 8] for n in range(8)]
    d = [None] + [b[n] - b[8 - n] for n in (1, 2, 3)]
    s = [None] + [b[n] + b[8 - n] for n in (1, 2, 3)]
    u, v = b[0] + c2 * d[2], b[0] - c2 * d[2]
    p, q = c1 * d[1] + c3 * d[3], c3 * d[1] - c1 * d[3]
    g, h = b[4] + c2 * s[2], b[4] - c2 * s[2]
    m, n = c3 * s[1] + c1 * s[3], c1 * s[1] - c3 * s[3]
    e = [a[n_] + a[n_ + 4] for n_ in range(4)]
    f = [a[n_] - a[n_ + 4] for n_ in range(4)]
    w, z = c2 * (f[1] - f[3]), c2 * (f[1] + f[3])
    even, odd = e[0] + e[2], e[1] + e[3]
    return [
        (even + odd, even - odd),
        (u + p, g + m),
        (f[0] + w, f[2] + z),
        (v + q, n - h),
        (e[0] - e[2], e[1] - e[3]),
        (v - q, h + n),
        (f[0] - w, z - f[2]),
        (u - p, m - g),
    ]


def filter_outputs(plan, fft_len, keep, sources, taps_ref, base_ref, out_ref, start):
    rows = sources[0].shape[0]

    @pl.loop(0, RADIX)
    def _(col):
        base = pl.multiple_of(col * LANES, LANES)
        lanes = pl.ds(base, LANES)
        weights = [jnp.broadcast_to(taps_ref[pl.ds(j, 1), lanes], (rows, LANES)) for j in range(taps_ref.shape[0])]
        for block in range(0, len(plan), BLOCK):
            held = {}
            for out in range(block, min(block + BLOCK, len(plan))):
                at = pl.ds((start + out) * rows, rows)
                sums = {False: None if base_ref is None else base_ref[at, lanes], True: None}
                for j, src, frame, wiped in plan[out]:
                    if (src, frame) not in held:
                        lane = pl.multiple_of(frame * fft_len + base, LANES)
                        held[src, frame] = sources[src][:, pl.ds(lane, LANES)].astype(jnp.float32)
                    term = held[src, frame] * weights[j]
                    sums[wiped] = term if sums[wiped] is None else sums[wiped] + term
                total = sums[False]
                if sums[True] is not None:
                    wiped_sum = jnp.where(keep, sums[True], 0.0)
                    total = wiped_sum if total is None else total + wiped_sum
                out_ref[at, lanes] = total


def first_steps(filt, rows, first, count, high, low, offset, unroll=1):
    @pl.loop(0, count, unroll=unroll)
    def _(out):
        at = pl.ds(pl.multiple_of((out + first) * rows, rows), rows)
        to = pl.ds(pl.multiple_of(out * rows + offset, rows), rows)
        parts = first_step([filt[at, n * LANES : (n + 1) * LANES] for n in range(RADIX)])
        for pair, halves in enumerate(parts):
            for k, value in enumerate(halves):
                top = value.astype(jnp.bfloat16)
                high[pair, to, k * LANES : (k + 1) * LANES] = top
                low[pair, to, k * LANES : (k + 1) * LANES] = (value - top.astype(jnp.float32)).astype(jnp.bfloat16)


def second_steps(table, high, low, turned, ready, out_ref, half, sems):
    quarter = PLANE * Z_HIGH * Z_LOW
    per_dev = 4
    z_size = Z_HIGH * Z_LOW
    block = 2 * per_dev
    share = z_size * block
    cols = ready.shape[1]

    def product(left, right):
        return lax.dot_general(left, right, (((1,), (1,)), ((), ())), preferred_element_type=jnp.float32)

    def send(first_y, count, sem):
        copies = []
        for plane in range(PLANE):
            at = pl.ds((plane * Y_SIZE + first_y) * share, count * share)
            for lane in range(cols // LANES):
                ready[at, lane * LANES : (lane + 1) * LANES] = turned[lane, at].astype(jnp.bfloat16)
            copies.append(
                pltpu.make_async_copy(ready.at[at], out_ref.at[at, pl.ds(half * cols, cols)], sems.at[sem + plane])
            )
            copies[-1].start()
        return copies

    size = 2 * LANES
    copies = []
    for pair in range(RADIX // 2):
        table_high, table_low = table[pair, :size], table[pair, size:]
        both = product(table[pair], high[pair])
        result = (both[size:] + product(table_high, low[pair])) + both[:size]
        for slot in range(2):
            kappa = (pair, RADIX - pair)[slot] if pair else (0, RADIX // 2)[slot]
            for part in range(2):
                for plane in range(PLANE):
                    first = slot * LANES + part * quarter + plane * z_size
                    row = (plane * Y_SIZE + kappa // per_dev) * share + (kappa % per_dev) * 2 + part
                    for lane in range(cols // LANES):
                        turned[lane, pl.ds(row, z_size, stride=block), :] = result[
                            first : first + z_size, lane * LANES : (lane + 1) * LANES
                        ]
        if pair == 4:
            copies += send(0, 1, 0) + send(3, 1, PLANE)
    copies += send(1, 2, 2 * PLANE)
    for copy in copies:
        copy.wait()


def middle_kernel(plan, own, fft_len, keep_ref, volts_hbm, taps_hbm, table_hbm, out_ref, more_high, more_low, partial,
                  taps, table, volts, filt, high, low, turned, ready, out_sems, sems):
    rows = volts.shape[0]
    keep = keep_ref[0] != 0
    frames = volts.shape[1] // fft_len
    copies = [pltpu.make_async_copy(taps_hbm, taps, sems.at[0])]
    bounds = (0, 15, 21, 27, frames)
    for piece in range(4):
        part = pl.ds(bounds[piece] * fft_len, (bounds[piece + 1] - bounds[piece]) * fft_len)
        copies.append(pltpu.make_async_copy(volts_hbm.at[:, part], volts.at[:, part], sems.at[1 + piece]))
    copies.append(pltpu.make_async_copy(table_hbm, table, sems.at[5]))
    for copy in copies:
        copy.start()
    copies[0].wait()
    done = 0
    for piece in range(4):
        copies[1 + piece].wait()
        upto = bounds[piece + 1] - (taps.shape[0] - 1)
        filter_outputs(plan[done:upto], fft_len, keep, [volts], taps, None, filt, done)
        done = upto
    filter_outputs(own, fft_len, keep, [volts], taps, None, partial, 0)
    first_steps(filt, rows, 0, HALF, high, low, 0)
    first_steps(filt, rows, HALF, len(plan) - HALF, more_high, more_low, 0)
    copies[5].wait()
    second_steps(table, high, low, turned, ready, out_ref, 0, out_sems)


def edge_kernel(plan, fft_len, taps, table, earlier, later, partial, more_high, more_low, _, out_ref,
                filt, high, low, turned, ready, out_sems, sems):
    rows = earlier.shape[0]
    copies = [
        pltpu.make_async_copy(more_high, high.at[:, pl.ds(0, more_high.shape[1])], sems.at[0]),
        pltpu.make_async_copy(more_low, low.at[:, pl.ds(0, more_low.shape[1])], sems.at[1]),
    ]
    for copy in copies:
        copy.start()
    filter_outputs(plan, fft_len, None, [earlier, later], taps, partial, filt, 0)
    first_steps(filt, rows, 0, len(plan), high, low, more_high.shape[1], len(plan))
    for copy in copies:
        copy.wait()
    second_steps(table, high, low, turned, ready, out_ref, 1, out_sems)


def spectra_scratch(rows, fft_len, outputs):
    cols = HALF * rows
    return [
        pltpu.VMEM((outputs * rows, fft_len), jnp.float32),
        pltpu.VMEM((RADIX // 2, cols, 2 * LANES), jnp.bfloat16),
        pltpu.VMEM((RADIX // 2, cols, 2 * LANES), jnp.bfloat16),
        pltpu.VMEM((cols // LANES, fft_len + 8, LANES), jnp.float32),
        pltpu.VMEM((fft_len, cols), jnp.bfloat16),
        pltpu.SemaphoreType.DMA((3 * PLANE,)),
    ]


def middle_call(plan, own, keep, volts, taps, table):
    rows, fft_len = volts.shape[0], taps.shape[1]
    cols = HALF * rows
    more = jax.ShapeDtypeStruct((RADIX // 2, (len(plan) - HALF) * rows, 2 * LANES), jnp.bfloat16)
    partial = jax.ShapeDtypeStruct((len(own) * rows, fft_len), jnp.float32)
    hbm = pl.BlockSpec(memory_space=pltpu.HBM)
    vmem = pl.BlockSpec(memory_space=pltpu.VMEM)
    return pl.pallas_call(
        functools.partial(middle_kernel, plan, own, fft_len),
        out_shape=(
            pltpu.HBM((fft_len, 2 * cols), jnp.bfloat16),
            *(pltpu.VMEM(x.shape, x.dtype) for x in (more, more, partial, taps, table)),
        ),
        in_specs=[pl.BlockSpec(memory_space=pltpu.SMEM), hbm, hbm, hbm],
        out_specs=(hbm, vmem, vmem, vmem, vmem, vmem),
        scratch_shapes=[pltpu.VMEM(volts.shape, volts.dtype)]
        + spectra_scratch(rows, fft_len, len(plan))
        + [pltpu.SemaphoreType.DMA((6,))],
        compiler_params=pltpu.CompilerParams(vmem_limit_bytes=VMEM_LIMIT),
        cost_estimate=pl.CostEstimate(flops=10**9, bytes_accessed=8 * 2**20, transcendentals=0),
        name="middle",
    )(keep, *(pltpu.with_memory_space_constraint(x, pltpu.HBM) for x in (volts, taps, table)))


def edge_call(plan, taps, table, earlier, later, partial, more_high, more_low, spectra):
    rows, fft_len = earlier.shape[0], taps.shape[1]
    hbm = pl.BlockSpec(memory_space=pltpu.HBM)
    vmem = pl.BlockSpec(memory_space=pltpu.VMEM)
    anywhere = pl.BlockSpec(memory_space=pl.ANY)
    return pl.pallas_call(
        functools.partial(edge_kernel, plan, fft_len),
        out_shape=pltpu.HBM(spectra.shape, spectra.dtype),
        in_specs=[vmem, vmem, vmem, vmem, vmem, anywhere, anywhere, hbm],
        out_specs=hbm,
        scratch_shapes=spectra_scratch(rows, fft_len, len(plan)) + [pltpu.SemaphoreType.DMA((2,))],
        input_output_aliases={7: 0},
        compiler_params=pltpu.CompilerParams(vmem_limit_bytes=VMEM_LIMIT),
        cost_estimate=pl.CostEstimate(flops=10**9, bytes_accessed=8 * 2**20, transcendentals=0),
        name="edge",
    )(
        taps, table, earlier, later, partial, more_high, more_low, spectra,
    )


def ends_kernel(volts, last_ref, first_ref, sems):
    size = last_ref.shape[1]
    copies = [
        pltpu.make_async_copy(volts.at[:, pl.ds(volts.shape[1] - size, size)], last_ref, sems.at[0]),
        pltpu.make_async_copy(volts.at[:, pl.ds(0, first_ref.shape[1])], first_ref, sems.at[1]),
    ]
    for copy in copies:
        copy.start()
    for copy in copies:
        copy.wait()


def ends_call(volts, last, first):
    vmem = pl.BlockSpec(memory_space=pltpu.VMEM)
    rows = volts.shape[0]
    return pl.pallas_call(
        ends_kernel,
        out_shape=(pltpu.VMEM((rows, last), volts.dtype), pltpu.VMEM((rows, first), volts.dtype)),
        in_specs=[pl.BlockSpec(memory_space=pltpu.HBM)],
        out_specs=(vmem, vmem),
        scratch_shapes=[pltpu.SemaphoreType.DMA((2,))],
        name="ends",
    )(pltpu.with_memory_space_constraint(volts, pltpu.HBM))


def gram_kernel(scale, pairs_ref, got_ref, out_ref, wide, both, tiles, sems):
    groups = wide.shape[0]
    per_src = 8
    times = Y_SIZE * Z_LOW
    inputs = LANES // 8
    pitch = 3 * per_src
    stations = Z_HIGH * PLANE * inputs

    copies = []
    for chan in range(out_ref.shape[1]):
        for stn in range(Z_HIGH * PLANE):
            if chan == 0 and stn < PLANE:
                for two in range(stn * times, (stn + 1) * times):
                    from_rows = pl.ds(two * 2 * per_src, 2 * per_src)
                    for group in range(groups):
                        wide[group, pl.ds(two * pitch, 2 * per_src)] = got_ref[
                            from_rows, group * LANES : (group + 1) * LANES
                        ].astype(jnp.float32)
            at = pl.ds(stn * inputs, inputs)
            turned_at = pl.ds(stations + stn * inputs, inputs)
            first = (stn % PLANE) * times * pitch + (stn // PLANE) * per_src + chan * 2
            parts = [
                [wide[group, pl.ds(first + part, times, stride=pitch), :] for group in range(groups)] for part in range(2)
            ]
            plain = jnp.concatenate(parts[0] + parts[1], 0).astype(jnp.bfloat16).T
            turned = jnp.concatenate([-v for v in parts[1]] + parts[0], 0).astype(jnp.bfloat16).T
            for t in range(LANES // inputs):
                cols = slice(t * LANES, (t + 1) * LANES)
                both[chan, at, cols] = plain[t * inputs : (t + 1) * inputs]
                both[chan, turned_at, cols] = turned[t * inputs : (t + 1) * inputs]
        sums = lax.dot_general(
            both[chan, :stations], both[chan], (((1,), (1,)), ((), ())), preferred_element_type=jnp.float32
        )
        for first in range(2):
            for second in range(2):
                for part in range(2):
                    col = part * stations + second * TILE
                    tiles[chan, first, second, part] = sums[first * TILE : (first + 1) * TILE, col : col + TILE] * scale
        for tile in range(pairs_ref.shape[0]):
            for part in range(2):
                copies.append(
                    pltpu.make_async_copy(
                        tiles.at[chan, pairs_ref[tile, 0], pairs_ref[tile, 1], part],
                        out_ref.at[part, chan, tile],
                        sems.at[len(copies)],
                    )
                )
                copies[-1].start()
    for copy in copies:
        copy.wait()


def gram_call(got, tile_pairs, chans, total_spectra):
    rows, lanes = got.shape
    stations = 2 * TILE
    depth = 8 * LANES
    tiles = tile_pairs.shape[0]
    return pl.pallas_call(
        functools.partial(gram_kernel, 1.0 / total_spectra),
        out_shape=jax.ShapeDtypeStruct((2, chans, tiles, TILE, TILE), jnp.float32),
        in_specs=[pl.BlockSpec(memory_space=pltpu.SMEM), pl.BlockSpec(memory_space=pltpu.VMEM)],
        out_specs=pl.BlockSpec(memory_space=pl.ANY),
        scratch_shapes=[
            pltpu.VMEM((lanes // LANES, rows // 2 * 3 + 24, LANES), jnp.float32),
            pltpu.VMEM((chans, 2 * stations, depth), jnp.bfloat16),
            pltpu.VMEM((chans, 2, 2, 2, TILE, TILE), jnp.float32),
            pltpu.SemaphoreType.DMA((2 * chans * tiles,)),
        ],
        compiler_params=pltpu.CompilerParams(vmem_limit_bytes=VMEM_LIMIT),
        name="grams",
    )(tile_pairs, got)


def plans(frames, tap_count):
    ahead = tap_count - 1 - BACK

    def taps(out):
        own, others = [], []
        for j in range(tap_count):
            frame = out - (tap_count - 1) + j
            if frame < 0:
                others.append((j, 0, frame + ahead, False))
            elif frame >= frames:
                others.append((j, 1, frame - frames, False))
            else:
                own.append((j, 0, frame, out >= frames))
        return own, others

    middle = [taps(out)[0] for out in range(tap_count - 1, frames)]
    edges = [taps(out) for out in [*range(BACK, tap_count - 1), *range(frames, frames + BACK)]]
    return middle, [own for own, _ in edges], [others for _, others in edges]


def shards(volts, taps, tile_pairs):
    tap_count, fft_len = taps.shape
    frames = volts.shape[1] // fft_len
    peers = lax.axis_size("tm")
    last, first = ends_call(volts, (tap_count - 1 - BACK) * fft_len, BACK * fft_len)
    earlier = lax.ppermute(last, "tm", [(i, i + 1) for i in range(peers - 1)])
    later = lax.ppermute(first, "tm", [(i, (i - 1) % peers) for i in range(peers)])
    table = jnp.asarray(second_step_table(fft_len))
    middle, own, others = plans(frames, tap_count)
    keep = (lax.axis_index("tm") != peers - 1).astype(jnp.int32).reshape(1)
    spectra, more_high, more_low, partial, taps, table = middle_call(middle, own, keep, volts, taps, table)
    spectra = edge_call(others, taps, table, earlier, later, partial, more_high, more_low, spectra)
    order = device_order()
    chans = fft_len // 2 // len(order)
    blocks = spectra.reshape(len(order), 2 * chans, spectra.shape[1])
    got = lax.all_to_all(
        blocks, ("stn", "tm"), split_axis=0, concat_axis=0, tiled=True, axis_index_groups=[order]
    )
    return gram_call(got.reshape(spectra.shape), tile_pairs, chans, frames * peers)


def solution(mesh):
    return jax.shard_map(
        shards,
        mesh=mesh,
        in_specs=(P("stn", "tm"), P(), P()),
        out_specs=P(None, ("stn", "tm"), None, None, None),
        check_vma=False,
    )
```

```python
import functools
import math

import jax
import jax.numpy as jnp
import ml_dtypes
import numpy as np
from jax import lax
from jax.experimental import pallas as pl
from jax.experimental.pallas import tpu as pltpu
from jax.sharding import PartitionSpec as P

TILE = 128
LANES = 128
RADIX = 16
BACK = 5
BLOCK = 2
HALF = 16
Z_HIGH, PLANE, Z_LOW, Y_SIZE = 2, 8, 4, 4
Z_LOW_ORDER = (0, 2, 1, 3)
VMEM_LIMIT = 48 * 1024 * 1024


def device_order():
    order = []
    for plane in range(PLANE):
        for y in range(Y_SIZE):
            for low in Z_LOW_ORDER:
                for high in range(Z_HIGH):
                    order.append(((high * PLANE + plane) * Z_LOW + low) * Y_SIZE + y)
    return order


def second_step_table(fft_len):
    length = fft_len // RADIX
    quarter = length // 2
    place = np.arange(length, dtype=np.int64)
    out = np.zeros((RADIX // 2, 2 * length, 2 * length), np.float64)
    column = np.array([dev // Y_SIZE for dev in device_order() if dev % Y_SIZE == 0], np.int64)

    def rows(kappa):
        chan = kappa + RADIX * column
        angle = 2.0 * np.pi * ((chan[:, None] * place[None, :]) % fft_len) / fft_len
        return np.cos(angle), np.sin(angle)

    for pair in range(RADIX // 2):
        for slot in range(2):
            if pair == 0:
                kappa = 0 if slot == 0 else RADIX // 2
            else:
                kappa = pair if slot == 0 else RADIX - pair
            cos, sin = rows(kappa)
            first = slot * length
            if pair == 0:
                cols = slice(slot * length, (slot + 1) * length)
                out[pair, first : first + quarter, cols] = cos
                out[pair, first + quarter : first + length, cols] = -sin
            else:
                sign = 1.0 if slot == 0 else -1.0
                out[pair, first : first + quarter, :length] = cos
                out[pair, first : first + quarter, length:] = -sign * sin
                out[pair, first + quarter : first + length, :length] = -sin
                out[pair, first + quarter : first + length, length:] = -sign * cos
    out = (out / math.sqrt(fft_len)).astype(np.float32)
    high = out.astype(ml_dtypes.bfloat16)
    low = (out - high.astype(np.float32)).astype(ml_dtypes.bfloat16)
    return np.concatenate([high, low], axis=1)


def first_step(x):
    c1, c2, c3 = (math.cos(math.pi * j / 8) for j in (1, 2, 3))
    a = [x[n] + x[n + 8] for n in range(8)]
    b = [x[n] - x[n + 8] for n in range(8)]
    d = [None] + [b[n] - b[8 - n] for n in (1, 2, 3)]
    s = [None] + [b[n] + b[8 - n] for n in (1, 2, 3)]
    u, v = b[0] + c2 * d[2], b[0] - c2 * d[2]
    p, q = c1 * d[1] + c3 * d[3], c3 * d[1] - c1 * d[3]
    g, h = b[4] + c2 * s[2], b[4] - c2 * s[2]
    m, n = c3 * s[1] + c1 * s[3], c1 * s[1] - c3 * s[3]
    e = [a[n_] + a[n_ + 4] for n_ in range(4)]
    f = [a[n_] - a[n_ + 4] for n_ in range(4)]
    w, z = c2 * (f[1] - f[3]), c2 * (f[1] + f[3])
    even, odd = e[0] + e[2], e[1] + e[3]
    return [
        (even + odd, even - odd),
        (u + p, g + m),
        (f[0] + w, f[2] + z),
        (v + q, n - h),
        (e[0] - e[2], e[1] - e[3]),
        (v - q, h + n),
        (f[0] - w, z - f[2]),
        (u - p, m - g),
    ]


def filter_outputs(plan, fft_len, keep, sources, taps_ref, base_ref, out_ref, start):
    rows = sources[0].shape[0]

    @pl.loop(0, RADIX)
    def _(col):
        base = pl.multiple_of(col * LANES, LANES)
        lanes = pl.ds(base, LANES)
        weights = [jnp.broadcast_to(taps_ref[pl.ds(j, 1), lanes], (rows, LANES)) for j in range(taps_ref.shape[0])]
        for block in range(0, len(plan), BLOCK):
            held = {}
            for out in range(block, min(block + BLOCK, len(plan))):
                at = pl.ds((start + out) * rows, rows)
                sums = {False: None if base_ref is None else base_ref[at, lanes], True: None}
                for j, src, frame, wiped in plan[out]:
                    if (src, frame) not in held:
                        lane = pl.multiple_of(frame * fft_len + base, LANES)
                        held[src, frame] = sources[src][:, pl.ds(lane, LANES)].astype(jnp.float32)
                    term = held[src, frame] * weights[j]
                    sums[wiped] = term if sums[wiped] is None else sums[wiped] + term
                total = sums[False]
                if sums[True] is not None:
                    wiped_sum = jnp.where(keep, sums[True], 0.0)
                    total = wiped_sum if total is None else total + wiped_sum
                out_ref[at, lanes] = total


def first_steps(filt, rows, first, count, high, low, offset, unroll=1):
    @pl.loop(0, count, unroll=unroll)
    def _(out):
        at = pl.ds(pl.multiple_of((out + first) * rows, rows), rows)
        to = pl.ds(pl.multiple_of(out * rows + offset, rows), rows)
        parts = first_step([filt[at, n * LANES : (n + 1) * LANES] for n in range(RADIX)])
        for pair, halves in enumerate(parts):
            for k, value in enumerate(halves):
                top = value.astype(jnp.bfloat16)
                high[pair, to, k * LANES : (k + 1) * LANES] = top
                low[pair, to, k * LANES : (k + 1) * LANES] = (value - top.astype(jnp.float32)).astype(jnp.bfloat16)


def second_steps(table, high, low, turned, ready, out_ref, half, sems):
    quarter = PLANE * Z_HIGH * Z_LOW
    per_dev = 4
    z_size = Z_HIGH * Z_LOW
    block = 2 * per_dev
    share = z_size * block
    cols = ready.shape[1]

    def product(left, right):
        return lax.dot_general(left, right, (((1,), (1,)), ((), ())), preferred_element_type=jnp.float32)

    def send(first_y, count, sem):
        copies = []
        for plane in range(PLANE):
            at = pl.ds((plane * Y_SIZE + first_y) * share, count * share)
            for lane in range(cols // LANES):
                ready[at, lane * LANES : (lane + 1) * LANES] = turned[lane, at].astype(jnp.bfloat16)
            copies.append(
                pltpu.make_async_copy(ready.at[at], out_ref.at[at, pl.ds(half * cols, cols)], sems.at[sem + plane])
            )
            copies[-1].start()
        return copies

    size = 2 * LANES
    copies = []
    for pair in range(RADIX // 2):
        table_high, table_low = table[pair, :size], table[pair, size:]
        both = product(table[pair], high[pair])
        result = (both[size:] + product(table_high, low[pair])) + both[:size]
        for slot in range(2):
            kappa = (pair, RADIX - pair)[slot] if pair else (0, RADIX // 2)[slot]
            for part in range(2):
                for plane in range(PLANE):
                    first = slot * LANES + part * quarter + plane * z_size
                    row = (plane * Y_SIZE + kappa // per_dev) * share + (kappa % per_dev) * 2 + part
                    for lane in range(cols // LANES):
                        turned[lane, pl.ds(row, z_size, stride=block), :] = result[
                            first : first + z_size, lane * LANES : (lane + 1) * LANES
                        ]
        if pair == 4:
            copies += send(0, 1, 0) + send(3, 1, PLANE)
    copies += send(1, 2, 2 * PLANE)
    for copy in copies:
        copy.wait()


def middle_kernel(plan, own, fft_len, pairs_hbm, volts_hbm, taps_hbm, table_hbm, out_ref, more_high, more_low,
                  partial, taps, table, pairs_out, volts, filt, high, low, turned, ready, out_sems, sems):
    rows = volts.shape[0]
    keep = lax.axis_index("tm") != lax.axis_size("tm") - 1
    frames = volts.shape[1] // fft_len
    copies = [pltpu.make_async_copy(taps_hbm, taps, sems.at[0])]
    bounds = (0, 15, 21, 27, frames)
    for piece in range(4):
        part = pl.ds(bounds[piece] * fft_len, (bounds[piece + 1] - bounds[piece]) * fft_len)
        copies.append(pltpu.make_async_copy(volts_hbm.at[:, part], volts.at[:, part], sems.at[1 + piece]))
    copies.append(pltpu.make_async_copy(table_hbm, table, sems.at[5]))
    copies.append(pltpu.make_async_copy(pairs_hbm, pairs_out, sems.at[6]))
    for copy in copies:
        copy.start()
    copies[0].wait()
    done = 0
    for piece in range(4):
        copies[1 + piece].wait()
        upto = bounds[piece + 1] - (taps.shape[0] - 1)
        filter_outputs(plan[done:upto], fft_len, keep, [volts], taps, None, filt, done)
        done = upto
    filter_outputs(own, fft_len, keep, [volts], taps, None, partial, 0)
    first_steps(filt, rows, 0, HALF, high, low, 0)
    first_steps(filt, rows, HALF, len(plan) - HALF, more_high, more_low, 0)
    copies[5].wait()
    copies[6].wait()
    second_steps(table, high, low, turned, ready, out_ref, 0, out_sems)


def edge_kernel(plan, fft_len, taps, table, earlier, later, partial, more_high, more_low, _, out_ref,
                filt, high, low, turned, ready, out_sems, sems):
    rows = earlier.shape[0]
    copies = [
        pltpu.make_async_copy(more_high, high.at[:, pl.ds(0, more_high.shape[1])], sems.at[0]),
        pltpu.make_async_copy(more_low, low.at[:, pl.ds(0, more_low.shape[1])], sems.at[1]),
    ]
    for copy in copies:
        copy.start()
    filter_outputs(plan, fft_len, None, [earlier, later], taps, partial, filt, 0)
    first_steps(filt, rows, 0, len(plan), high, low, more_high.shape[1], len(plan))
    for copy in copies:
        copy.wait()
    second_steps(table, high, low, turned, ready, out_ref, 1, out_sems)


def spectra_scratch(rows, fft_len, outputs):
    cols = HALF * rows
    return [
        pltpu.VMEM((outputs * rows, fft_len), jnp.float32),
        pltpu.VMEM((RADIX // 2, cols, 2 * LANES), jnp.bfloat16),
        pltpu.VMEM((RADIX // 2, cols, 2 * LANES), jnp.bfloat16),
        pltpu.VMEM((cols // LANES, fft_len + 8, LANES), jnp.float32),
        pltpu.VMEM((fft_len, cols), jnp.bfloat16),
        pltpu.SemaphoreType.DMA((3 * PLANE,)),
    ]


def middle_call(plan, own, tile_pairs, volts, taps, table):
    rows, fft_len = volts.shape[0], taps.shape[1]
    cols = HALF * rows
    more = jax.ShapeDtypeStruct((RADIX // 2, (len(plan) - HALF) * rows, 2 * LANES), jnp.bfloat16)
    partial = jax.ShapeDtypeStruct((len(own) * rows, fft_len), jnp.float32)
    hbm = pl.BlockSpec(memory_space=pltpu.HBM)
    vmem = pl.BlockSpec(memory_space=pltpu.VMEM)
    smem = pl.BlockSpec(memory_space=pltpu.SMEM)
    return pl.pallas_call(
        functools.partial(middle_kernel, plan, own, fft_len),
        out_shape=(
            pltpu.HBM((fft_len, 2 * cols), jnp.bfloat16),
            *(pltpu.VMEM(x.shape, x.dtype) for x in (more, more, partial, taps, table)),
            pltpu.SMEM(tile_pairs.shape, tile_pairs.dtype),
        ),
        in_specs=[hbm, hbm, hbm, hbm],
        out_specs=(hbm, vmem, vmem, vmem, vmem, vmem, smem),
        scratch_shapes=[pltpu.VMEM(volts.shape, volts.dtype)]
        + spectra_scratch(rows, fft_len, len(plan))
        + [pltpu.SemaphoreType.DMA((7,))],
        compiler_params=pltpu.CompilerParams(vmem_limit_bytes=VMEM_LIMIT),
        cost_estimate=pl.CostEstimate(flops=10**9, bytes_accessed=8 * 2**20, transcendentals=0),
        name="middle",
    )(*(pltpu.with_memory_space_constraint(x, pltpu.HBM) for x in (tile_pairs, volts, taps, table)))


def edge_call(plan, taps, table, earlier, later, partial, more_high, more_low, spectra):
    rows, fft_len = earlier.shape[0], taps.shape[1]
    hbm = pl.BlockSpec(memory_space=pltpu.HBM)
    vmem = pl.BlockSpec(memory_space=pltpu.VMEM)
    anywhere = pl.BlockSpec(memory_space=pl.ANY)
    return pl.pallas_call(
        functools.partial(edge_kernel, plan, fft_len),
        out_shape=pltpu.HBM(spectra.shape, spectra.dtype),
        in_specs=[vmem, vmem, vmem, vmem, vmem, anywhere, anywhere, hbm],
        out_specs=hbm,
        scratch_shapes=spectra_scratch(rows, fft_len, len(plan)) + [pltpu.SemaphoreType.DMA((2,))],
        input_output_aliases={7: 0},
        compiler_params=pltpu.CompilerParams(vmem_limit_bytes=VMEM_LIMIT),
        cost_estimate=pl.CostEstimate(flops=10**9, bytes_accessed=8 * 2**20, transcendentals=0),
        name="edge",
    )(
        taps, table, earlier, later, partial, more_high, more_low, spectra,
    )


def ends_kernel(volts, last_ref, first_ref, sems):
    size = last_ref.shape[1]
    copies = [
        pltpu.make_async_copy(volts.at[:, pl.ds(volts.shape[1] - size, size)], last_ref, sems.at[0]),
        pltpu.make_async_copy(volts.at[:, pl.ds(0, first_ref.shape[1])], first_ref, sems.at[1]),
    ]
    for copy in copies:
        copy.start()
    for copy in copies:
        copy.wait()


def ends_call(volts, last, first):
    vmem = pl.BlockSpec(memory_space=pltpu.VMEM)
    rows = volts.shape[0]
    return pl.pallas_call(
        ends_kernel,
        out_shape=(pltpu.VMEM((rows, last), volts.dtype), pltpu.VMEM((rows, first), volts.dtype)),
        in_specs=[pl.BlockSpec(memory_space=pltpu.HBM)],
        out_specs=(vmem, vmem),
        scratch_shapes=[pltpu.SemaphoreType.DMA((2,))],
        name="ends",
    )(pltpu.with_memory_space_constraint(volts, pltpu.HBM))


def gram_kernel(scale, pairs_ref, got_ref, out_ref, wide, both, tiles, sems):
    groups = wide.shape[0]
    per_src = 8
    times = Y_SIZE * Z_LOW
    inputs = LANES // 8
    pitch = 3 * per_src
    stations = Z_HIGH * PLANE * inputs

    copies = []
    for chan in range(out_ref.shape[1]):
        for stn in range(Z_HIGH * PLANE):
            if chan == 0 and stn < PLANE:
                for two in range(stn * times, (stn + 1) * times):
                    from_rows = pl.ds(two * 2 * per_src, 2 * per_src)
                    for group in range(groups):
                        wide[group, pl.ds(two * pitch, 2 * per_src)] = got_ref[
                            from_rows, group * LANES : (group + 1) * LANES
                        ].astype(jnp.float32)
            at = pl.ds(stn * inputs, inputs)
            turned_at = pl.ds(stations + stn * inputs, inputs)
            first = (stn % PLANE) * times * pitch + (stn // PLANE) * per_src + chan * 2
            parts = [
                [wide[group, pl.ds(first + part, times, stride=pitch), :] for group in range(groups)] for part in range(2)
            ]
            plain = jnp.concatenate(parts[0] + parts[1], 0).astype(jnp.bfloat16).T
            turned = jnp.concatenate([-v for v in parts[1]] + parts[0], 0).astype(jnp.bfloat16).T
            for t in range(LANES // inputs):
                cols = slice(t * LANES, (t + 1) * LANES)
                both[chan, at, cols] = plain[t * inputs : (t + 1) * inputs]
                both[chan, turned_at, cols] = turned[t * inputs : (t + 1) * inputs]
        sums = lax.dot_general(
            both[chan, :stations], both[chan], (((1,), (1,)), ((), ())), preferred_element_type=jnp.float32
        )
        for first in range(2):
            for second in range(2):
                for part in range(2):
                    col = part * stations + second * TILE
                    tiles[chan, first, second, part] = sums[first * TILE : (first + 1) * TILE, col : col + TILE] * scale
        for tile in range(pairs_ref.shape[1]):
            for part in range(2):
                copies.append(
                    pltpu.make_async_copy(
                        tiles.at[chan, pairs_ref[0, tile], pairs_ref[1, tile], part],
                        out_ref.at[part, chan, tile],
                        sems.at[len(copies)],
                    )
                )
                copies[-1].start()
    for copy in copies:
        copy.wait()


def gram_call(got, tile_pairs, chans, total_spectra):
    rows, lanes = got.shape
    stations = 2 * TILE
    depth = 8 * LANES
    tiles = tile_pairs.shape[1]
    return pl.pallas_call(
        functools.partial(gram_kernel, 1.0 / total_spectra),
        out_shape=jax.ShapeDtypeStruct((2, chans, tiles, TILE, TILE), jnp.float32),
        in_specs=[pl.BlockSpec(memory_space=pltpu.SMEM), pl.BlockSpec(memory_space=pltpu.VMEM)],
        out_specs=pl.BlockSpec(memory_space=pl.ANY),
        scratch_shapes=[
            pltpu.VMEM((lanes // LANES, rows // 2 * 3 + 24, LANES), jnp.float32),
            pltpu.VMEM((chans, 2 * stations, depth), jnp.bfloat16),
            pltpu.VMEM((chans, 2, 2, 2, TILE, TILE), jnp.float32),
            pltpu.SemaphoreType.DMA((2 * chans * tiles,)),
        ],
        compiler_params=pltpu.CompilerParams(vmem_limit_bytes=VMEM_LIMIT),
        name="grams",
    )(tile_pairs, got)


def plans(frames, tap_count):
    ahead = tap_count - 1 - BACK

    def taps(out):
        own, others = [], []
        for j in range(tap_count):
            frame = out - (tap_count - 1) + j
            if frame < 0:
                others.append((j, 0, frame + ahead, False))
            elif frame >= frames:
                others.append((j, 1, frame - frames, False))
            else:
                own.append((j, 0, frame, out >= frames))
        return own, others

    middle = [taps(out)[0] for out in range(tap_count - 1, frames)]
    edges = [taps(out) for out in [*range(BACK, tap_count - 1), *range(frames, frames + BACK)]]
    return middle, [own for own, _ in edges], [others for _, others in edges]


def shards(volts, taps, tile_pairs):
    tap_count, fft_len = taps.shape
    frames = volts.shape[1] // fft_len
    peers = lax.axis_size("tm")
    last, first = ends_call(volts, (tap_count - 1 - BACK) * fft_len, BACK * fft_len)
    earlier = lax.ppermute(last, "tm", [(i, i + 1) for i in range(peers - 1)])
    later = lax.ppermute(first, "tm", [(i, (i - 1) % peers) for i in range(peers)])
    table = jnp.asarray(second_step_table(fft_len))
    middle, own, others = plans(frames, tap_count)
    spectra, more_high, more_low, partial, taps, table, pairs = middle_call(middle, own, tile_pairs.T, volts, taps, table)
    spectra = edge_call(others, taps, table, earlier, later, partial, more_high, more_low, spectra)
    order = device_order()
    chans = fft_len // 2 // len(order)
    blocks = spectra.reshape(len(order), 2 * chans, spectra.shape[1])
    got = lax.all_to_all(
        blocks, ("stn", "tm"), split_axis=0, concat_axis=0, tiled=True, axis_index_groups=[order]
    )
    return gram_call(got.reshape(spectra.shape), pairs, chans, frames * peers)


def solution(mesh):
    return jax.shard_map(
        shards,
        mesh=mesh,
        in_specs=(P("stn", "tm"), P(), P()),
        out_specs=P(None, ("stn", "tm"), None, None, None),
        check_vma=False,
    )
```

```python
import functools
import math

import jax
import jax.numpy as jnp
import ml_dtypes
import numpy as np
from jax import lax
from jax.experimental import pallas as pl
from jax.experimental.pallas import tpu as pltpu
from jax.sharding import PartitionSpec as P

TILE = 128
LANES = 128
RADIX = 16
BACK = 5
BLOCK = 2
HALF = 16
Z_HIGH, PLANE, Z_LOW, Y_SIZE = 2, 8, 4, 4
Z_LOW_ORDER = (0, 2, 1, 3)
VMEM_LIMIT = 48 * 1024 * 1024


def device_order():
    order = []
    for plane in range(PLANE):
        for y in range(Y_SIZE):
            for low in Z_LOW_ORDER:
                for high in range(Z_HIGH):
                    order.append(((high * PLANE + plane) * Z_LOW + low) * Y_SIZE + y)
    return order


def second_step_table(fft_len):
    length = fft_len // RADIX
    quarter = length // 2
    place = np.arange(length, dtype=np.int64)
    out = np.zeros((RADIX // 2, 2 * length, 2 * length), np.float64)
    column = np.array([dev // Y_SIZE for dev in device_order() if dev % Y_SIZE == 0], np.int64)

    def rows(kappa):
        chan = kappa + RADIX * column
        angle = 2.0 * np.pi * ((chan[:, None] * place[None, :]) % fft_len) / fft_len
        return np.cos(angle), np.sin(angle)

    for pair in range(RADIX // 2):
        for slot in range(2):
            if pair == 0:
                kappa = 0 if slot == 0 else RADIX // 2
            else:
                kappa = pair if slot == 0 else RADIX - pair
            cos, sin = rows(kappa)
            first = slot * length
            if pair == 0:
                cols = slice(slot * length, (slot + 1) * length)
                out[pair, first : first + quarter, cols] = cos
                out[pair, first + quarter : first + length, cols] = -sin
            else:
                sign = 1.0 if slot == 0 else -1.0
                out[pair, first : first + quarter, :length] = cos
                out[pair, first : first + quarter, length:] = -sign * sin
                out[pair, first + quarter : first + length, :length] = -sin
                out[pair, first + quarter : first + length, length:] = -sign * cos
    out = (out / math.sqrt(fft_len)).astype(np.float32)
    high = out.astype(ml_dtypes.bfloat16)
    low = (out - high.astype(np.float32)).astype(ml_dtypes.bfloat16)
    return np.concatenate([high, low], axis=1)


def first_step(x):
    c1, c2, c3 = (math.cos(math.pi * j / 8) for j in (1, 2, 3))
    a = [x[n] + x[n + 8] for n in range(8)]
    b = [x[n] - x[n + 8] for n in range(8)]
    d = [None] + [b[n] - b[8 - n] for n in (1, 2, 3)]
    s = [None] + [b[n] + b[8 - n] for n in (1, 2, 3)]
    u, v = b[0] + c2 * d[2], b[0] - c2 * d[2]
    p, q = c1 * d[1] + c3 * d[3], c3 * d[1] - c1 * d[3]
    g, h = b[4] + c2 * s[2], b[4] - c2 * s[2]
    m, n = c3 * s[1] + c1 * s[3], c1 * s[1] - c3 * s[3]
    e = [a[n_] + a[n_ + 4] for n_ in range(4)]
    f = [a[n_] - a[n_ + 4] for n_ in range(4)]
    w, z = c2 * (f[1] - f[3]), c2 * (f[1] + f[3])
    even, odd = e[0] + e[2], e[1] + e[3]
    return [
        (even + odd, even - odd),
        (u + p, g + m),
        (f[0] + w, f[2] + z),
        (v + q, n - h),
        (e[0] - e[2], e[1] - e[3]),
        (v - q, h + n),
        (f[0] - w, z - f[2]),
        (u - p, m - g),
    ]


def filter_outputs(plan, fft_len, keep, sources, taps_ref, base_ref, out_ref, start):
    rows = sources[0].shape[0]

    @pl.loop(0, RADIX)
    def _(col):
        base = pl.multiple_of(col * LANES, LANES)
        lanes = pl.ds(base, LANES)
        weights = [jnp.broadcast_to(taps_ref[pl.ds(j, 1), lanes], (rows, LANES)) for j in range(taps_ref.shape[0])]
        for block in range(0, len(plan), BLOCK):
            held = {}
            for out in range(block, min(block + BLOCK, len(plan))):
                at = pl.ds((start + out) * rows, rows)
                sums = {False: None if base_ref is None else base_ref[at, lanes], True: None}
                for j, src, frame, wiped in plan[out]:
                    if (src, frame) not in held:
                        lane = pl.multiple_of(frame * fft_len + base, LANES)
                        held[src, frame] = sources[src][:, pl.ds(lane, LANES)].astype(jnp.float32)
                    term = held[src, frame] * weights[j]
                    sums[wiped] = term if sums[wiped] is None else sums[wiped] + term
                total = sums[False]
                if sums[True] is not None:
                    wiped_sum = jnp.where(keep, sums[True], 0.0)
                    total = wiped_sum if total is None else total + wiped_sum
                out_ref[at, lanes] = total


def first_steps(filt, rows, first, count, high, low, offset, unroll=1):
    @pl.loop(0, count, unroll=unroll)
    def _(out):
        at = pl.ds(pl.multiple_of((out + first) * rows, rows), rows)
        to = pl.ds(pl.multiple_of(out * rows + offset, rows), rows)
        parts = first_step([filt[at, n * LANES : (n + 1) * LANES] for n in range(RADIX)])
        for pair, halves in enumerate(parts):
            for k, value in enumerate(halves):
                top = value.astype(jnp.bfloat16)
                high[pair, to, k * LANES : (k + 1) * LANES] = top
                low[pair, to, k * LANES : (k + 1) * LANES] = (value - top.astype(jnp.float32)).astype(jnp.bfloat16)


def second_steps(table, high, low, turned, ready, out_ref, half, sems):
    quarter = PLANE * Z_HIGH * Z_LOW
    per_dev = 4
    z_size = Z_HIGH * Z_LOW
    block = 2 * per_dev
    share = z_size * block
    cols = ready.shape[1]

    def product(left, right):
        return lax.dot_general(left, right, (((1,), (1,)), ((), ())), preferred_element_type=jnp.float32)

    def send(first_y, count, sem):
        copies = []
        for plane in range(PLANE):
            at = pl.ds((plane * Y_SIZE + first_y) * share, count * share)
            for lane in range(cols // LANES):
                ready[at, lane * LANES : (lane + 1) * LANES] = turned[lane, at].astype(jnp.bfloat16)
            copies.append(
                pltpu.make_async_copy(ready.at[at], out_ref.at[at, pl.ds(half * cols, cols)], sems.at[sem + plane])
            )
            copies[-1].start()
        return copies

    size = 2 * LANES
    copies = []
    for pair in range(RADIX // 2):
        table_high, table_low = table[pair, :size], table[pair, size:]
        both = product(table[pair], high[pair])
        result = (both[size:] + product(table_high, low[pair])) + both[:size]
        for slot in range(2):
            kappa = (pair, RADIX - pair)[slot] if pair else (0, RADIX // 2)[slot]
            for part in range(2):
                for plane in range(PLANE):
                    first = slot * LANES + part * quarter + plane * z_size
                    row = (plane * Y_SIZE + kappa // per_dev) * share + (kappa % per_dev) * 2 + part
                    for lane in range(cols // LANES):
                        turned[lane, pl.ds(row, z_size, stride=block), :] = result[
                            first : first + z_size, lane * LANES : (lane + 1) * LANES
                        ]
        if pair == 3:
            copies += send(0, 1, 0)
        if pair == 4:
            copies += send(3, 1, PLANE)
    return copies + send(1, 2, 2 * PLANE)


def middle_kernel(plan, own, fft_len, pairs_hbm, volts_hbm, taps_hbm, table_hbm, out_ref, more_high, more_low,
                  partial, taps, table, pairs_out, volts, filt, high, low, turned, ready, out_sems, sems):
    rows = volts.shape[0]
    keep = lax.axis_index("tm") != lax.axis_size("tm") - 1
    frames = volts.shape[1] // fft_len
    copies = [pltpu.make_async_copy(taps_hbm, taps, sems.at[0])]
    bounds = (0, 15, 21, 27, frames)
    for piece in range(4):
        part = pl.ds(bounds[piece] * fft_len, (bounds[piece + 1] - bounds[piece]) * fft_len)
        copies.append(pltpu.make_async_copy(volts_hbm.at[:, part], volts.at[:, part], sems.at[1 + piece]))
    copies.append(pltpu.make_async_copy(table_hbm, table, sems.at[5]))
    copies.append(pltpu.make_async_copy(pairs_hbm, pairs_out, sems.at[6]))
    for copy in copies:
        copy.start()
    copies[0].wait()
    done = 0
    for piece in range(4):
        copies[1 + piece].wait()
        upto = bounds[piece + 1] - (taps.shape[0] - 1)
        filter_outputs(plan[done:upto], fft_len, keep, [volts], taps, None, filt, done)
        done = upto
    first_steps(filt, rows, 0, HALF, high, low, 0)
    copies[5].wait()
    sent = second_steps(table, high, low, turned, ready, out_ref, 0, out_sems)
    filter_outputs(own, fft_len, keep, [volts], taps, None, partial, 0)
    first_steps(filt, rows, HALF, len(plan) - HALF, more_high, more_low, 0)
    for copy in [copies[6], *sent]:
        copy.wait()


def edge_kernel(plan, fft_len, taps, table, earlier, later, partial, more_high, more_low, _, out_ref,
                filt, high, low, turned, ready, out_sems, sems):
    rows = earlier.shape[0]
    copies = [
        pltpu.make_async_copy(more_high, high.at[:, pl.ds(0, more_high.shape[1])], sems.at[0]),
        pltpu.make_async_copy(more_low, low.at[:, pl.ds(0, more_low.shape[1])], sems.at[1]),
    ]
    for copy in copies:
        copy.start()
    filter_outputs(plan, fft_len, None, [earlier, later], taps, partial, filt, 0)
    first_steps(filt, rows, 0, len(plan), high, low, more_high.shape[1], len(plan))
    for copy in copies:
        copy.wait()
    for copy in second_steps(table, high, low, turned, ready, out_ref, 1, out_sems):
        copy.wait()


def spectra_scratch(rows, fft_len, outputs):
    cols = HALF * rows
    return [
        pltpu.VMEM((outputs * rows, fft_len), jnp.float32),
        pltpu.VMEM((RADIX // 2, cols, 2 * LANES), jnp.bfloat16),
        pltpu.VMEM((RADIX // 2, cols, 2 * LANES), jnp.bfloat16),
        pltpu.VMEM((cols // LANES, fft_len + 8, LANES), jnp.float32),
        pltpu.VMEM((fft_len, cols), jnp.bfloat16),
        pltpu.SemaphoreType.DMA((3 * PLANE,)),
    ]


def middle_call(plan, own, tile_pairs, volts, taps, table):
    rows, fft_len = volts.shape[0], taps.shape[1]
    cols = HALF * rows
    more = jax.ShapeDtypeStruct((RADIX // 2, (len(plan) - HALF) * rows, 2 * LANES), jnp.bfloat16)
    partial = jax.ShapeDtypeStruct((len(own) * rows, fft_len), jnp.float32)
    hbm = pl.BlockSpec(memory_space=pltpu.HBM)
    vmem = pl.BlockSpec(memory_space=pltpu.VMEM)
    smem = pl.BlockSpec(memory_space=pltpu.SMEM)
    return pl.pallas_call(
        functools.partial(middle_kernel, plan, own, fft_len),
        out_shape=(
            pltpu.HBM((fft_len, 2 * cols), jnp.bfloat16),
            *(pltpu.VMEM(x.shape, x.dtype) for x in (more, more, partial, taps, table)),
            pltpu.SMEM(tile_pairs.shape, tile_pairs.dtype),
        ),
        in_specs=[hbm, hbm, hbm, hbm],
        out_specs=(hbm, vmem, vmem, vmem, vmem, vmem, smem),
        scratch_shapes=[pltpu.VMEM(volts.shape, volts.dtype)]
        + spectra_scratch(rows, fft_len, len(plan))
        + [pltpu.SemaphoreType.DMA((7,))],
        compiler_params=pltpu.CompilerParams(vmem_limit_bytes=VMEM_LIMIT),
        cost_estimate=pl.CostEstimate(flops=10**9, bytes_accessed=8 * 2**20, transcendentals=0),
        name="middle",
    )(*(pltpu.with_memory_space_constraint(x, pltpu.HBM) for x in (tile_pairs, volts, taps, table)))


def edge_call(plan, taps, table, earlier, later, partial, more_high, more_low, spectra):
    rows, fft_len = earlier.shape[0], taps.shape[1]
    hbm = pl.BlockSpec(memory_space=pltpu.HBM)
    vmem = pl.BlockSpec(memory_space=pltpu.VMEM)
    anywhere = pl.BlockSpec(memory_space=pl.ANY)
    return pl.pallas_call(
        functools.partial(edge_kernel, plan, fft_len),
        out_shape=pltpu.HBM(spectra.shape, spectra.dtype),
        in_specs=[vmem, vmem, vmem, vmem, vmem, anywhere, anywhere, hbm],
        out_specs=hbm,
        scratch_shapes=spectra_scratch(rows, fft_len, len(plan)) + [pltpu.SemaphoreType.DMA((2,))],
        input_output_aliases={7: 0},
        compiler_params=pltpu.CompilerParams(vmem_limit_bytes=VMEM_LIMIT),
        cost_estimate=pl.CostEstimate(flops=10**9, bytes_accessed=8 * 2**20, transcendentals=0),
        name="edge",
    )(
        taps, table, earlier, later, partial, more_high, more_low, spectra,
    )


def ends_kernel(volts, last_ref, first_ref, sems):
    size = last_ref.shape[1]
    copies = [
        pltpu.make_async_copy(volts.at[:, pl.ds(volts.shape[1] - size, size)], last_ref, sems.at[0]),
        pltpu.make_async_copy(volts.at[:, pl.ds(0, first_ref.shape[1])], first_ref, sems.at[1]),
    ]
    for copy in copies:
        copy.start()
    for copy in copies:
        copy.wait()


def ends_call(volts, last, first):
    vmem = pl.BlockSpec(memory_space=pltpu.VMEM)
    rows = volts.shape[0]
    return pl.pallas_call(
        ends_kernel,
        out_shape=(pltpu.VMEM((rows, last), volts.dtype), pltpu.VMEM((rows, first), volts.dtype)),
        in_specs=[pl.BlockSpec(memory_space=pltpu.HBM)],
        out_specs=(vmem, vmem),
        scratch_shapes=[pltpu.SemaphoreType.DMA((2,))],
        name="ends",
    )(pltpu.with_memory_space_constraint(volts, pltpu.HBM))


def gram_kernel(scale, pairs_ref, got_ref, out_ref, wide, both, tiles, sems):
    groups = wide.shape[0]
    per_src = 8
    times = Y_SIZE * Z_LOW
    inputs = LANES // 8
    pitch = 3 * per_src
    stations = Z_HIGH * PLANE * inputs

    copies = []
    for chan in range(out_ref.shape[1]):
        for stn in range(Z_HIGH * PLANE):
            if chan == 0 and stn < PLANE:
                for two in range(stn * times, (stn + 1) * times):
                    from_rows = pl.ds(two * 2 * per_src, 2 * per_src)
                    for group in range(groups):
                        wide[group, pl.ds(two * pitch, 2 * per_src)] = got_ref[
                            from_rows, group * LANES : (group + 1) * LANES
                        ].astype(jnp.float32)
            at = pl.ds(stn * inputs, inputs)
            turned_at = pl.ds(stations + stn * inputs, inputs)
            first = (stn % PLANE) * times * pitch + (stn // PLANE) * per_src + chan * 2
            parts = [
                [wide[group, pl.ds(first + part, times, stride=pitch), :] for group in range(groups)] for part in range(2)
            ]
            plain = jnp.concatenate(parts[0] + parts[1], 0).astype(jnp.bfloat16).T
            turned = jnp.concatenate([-v for v in parts[1]] + parts[0], 0).astype(jnp.bfloat16).T
            for t in range(LANES // inputs):
                cols = slice(t * LANES, (t + 1) * LANES)
                both[chan, at, cols] = plain[t * inputs : (t + 1) * inputs]
                both[chan, turned_at, cols] = turned[t * inputs : (t + 1) * inputs]
        sums = lax.dot_general(
            both[chan, :stations], both[chan], (((1,), (1,)), ((), ())), preferred_element_type=jnp.float32
        )
        for first in range(2):
            for second in range(2):
                for part in range(2):
                    col = part * stations + second * TILE
                    tiles[chan, first, second, part] = sums[first * TILE : (first + 1) * TILE, col : col + TILE] * scale
        for tile in range(pairs_ref.shape[1]):
            for part in range(2):
                copies.append(
                    pltpu.make_async_copy(
                        tiles.at[chan, pairs_ref[0, tile], pairs_ref[1, tile], part],
                        out_ref.at[part, chan, tile],
                        sems.at[len(copies)],
                    )
                )
                copies[-1].start()
    for copy in copies:
        copy.wait()


def gram_call(got, tile_pairs, chans, total_spectra):
    rows, lanes = got.shape
    stations = 2 * TILE
    depth = 8 * LANES
    tiles = tile_pairs.shape[1]
    return pl.pallas_call(
        functools.partial(gram_kernel, 1.0 / total_spectra),
        out_shape=jax.ShapeDtypeStruct((2, chans, tiles, TILE, TILE), jnp.float32),
        in_specs=[pl.BlockSpec(memory_space=pltpu.SMEM), pl.BlockSpec(memory_space=pltpu.VMEM)],
        out_specs=pl.BlockSpec(memory_space=pl.ANY),
        scratch_shapes=[
            pltpu.VMEM((lanes // LANES, rows // 2 * 3 + 24, LANES), jnp.float32),
            pltpu.VMEM((chans, 2 * stations, depth), jnp.bfloat16),
            pltpu.VMEM((chans, 2, 2, 2, TILE, TILE), jnp.float32),
            pltpu.SemaphoreType.DMA((2 * chans * tiles,)),
        ],
        compiler_params=pltpu.CompilerParams(vmem_limit_bytes=VMEM_LIMIT),
        name="grams",
    )(tile_pairs, got)


def plans(frames, tap_count):
    ahead = tap_count - 1 - BACK

    def taps(out):
        own, others = [], []
        for j in range(tap_count):
            frame = out - (tap_count - 1) + j
            if frame < 0:
                others.append((j, 0, frame + ahead, False))
            elif frame >= frames:
                others.append((j, 1, frame - frames, False))
            else:
                own.append((j, 0, frame, out >= frames))
        return own, others

    middle = [taps(out)[0] for out in range(tap_count - 1, frames)]
    edges = [taps(out) for out in [*range(BACK, tap_count - 1), *range(frames, frames + BACK)]]
    return middle, [own for own, _ in edges], [others for _, others in edges]


def shards(volts, taps, tile_pairs):
    tap_count, fft_len = taps.shape
    frames = volts.shape[1] // fft_len
    peers = lax.axis_size("tm")
    last, first = ends_call(volts, (tap_count - 1 - BACK) * fft_len, BACK * fft_len)
    earlier = lax.ppermute(last, "tm", [(i, i + 1) for i in range(peers - 1)])
    later = lax.ppermute(first, "tm", [(i, (i - 1) % peers) for i in range(peers)])
    table = jnp.asarray(second_step_table(fft_len))
    middle, own, others = plans(frames, tap_count)
    spectra, more_high, more_low, partial, taps, table, pairs = middle_call(middle, own, tile_pairs.T, volts, taps, table)
    spectra = edge_call(others, taps, table, earlier, later, partial, more_high, more_low, spectra)
    order = device_order()
    chans = fft_len // 2 // len(order)
    blocks = spectra.reshape(len(order), 2 * chans, spectra.shape[1])
    got = lax.all_to_all(
        blocks, ("stn", "tm"), split_axis=0, concat_axis=0, tiled=True, axis_index_groups=[order]
    )
    return gram_call(got.reshape(spectra.shape), pairs, chans, frames * peers)


def solution(mesh):
    return jax.shard_map(
        shards,
        mesh=mesh,
        in_specs=(P("stn", "tm"), P(), P()),
        out_specs=P(None, ("stn", "tm"), None, None, None),
        check_vma=False,
    )
```

```python
import functools
import math

import jax
import jax.numpy as jnp
import ml_dtypes
import numpy as np
from jax import lax
from jax.experimental import pallas as pl
from jax.experimental.pallas import tpu as pltpu
from jax.sharding import PartitionSpec as P

TILE = 128
LANES = 128
RADIX = 16
BACK = 5
BLOCK = 2
HALF = 16
Z_HIGH, PLANE, Z_LOW, Y_SIZE = 2, 8, 4, 4
Z_LOW_ORDER = (0, 2, 1, 3)
ENDS_PIECE = 4096
VMEM_LIMIT = 48 * 1024 * 1024


def device_order():
    order = []
    for plane in range(PLANE):
        for y in range(Y_SIZE):
            for low in Z_LOW_ORDER:
                for high in range(Z_HIGH):
                    order.append(((high * PLANE + plane) * Z_LOW + low) * Y_SIZE + y)
    return order


def second_step_table(fft_len):
    length = fft_len // RADIX
    quarter = length // 2
    place = np.arange(length, dtype=np.int64)
    out = np.zeros((RADIX // 2, 2 * length, 2 * length), np.float64)
    column = np.array([dev // Y_SIZE for dev in device_order() if dev % Y_SIZE == 0], np.int64)

    def rows(kappa):
        chan = kappa + RADIX * column
        angle = 2.0 * np.pi * ((chan[:, None] * place[None, :]) % fft_len) / fft_len
        return np.cos(angle), np.sin(angle)

    for pair in range(RADIX // 2):
        for slot in range(2):
            if pair == 0:
                kappa = 0 if slot == 0 else RADIX // 2
            else:
                kappa = pair if slot == 0 else RADIX - pair
            cos, sin = rows(kappa)
            first = slot * length
            if pair == 0:
                cols = slice(slot * length, (slot + 1) * length)
                out[pair, first : first + quarter, cols] = cos
                out[pair, first + quarter : first + length, cols] = -sin
            else:
                sign = 1.0 if slot == 0 else -1.0
                out[pair, first : first + quarter, :length] = cos
                out[pair, first : first + quarter, length:] = -sign * sin
                out[pair, first + quarter : first + length, :length] = -sin
                out[pair, first + quarter : first + length, length:] = -sign * cos
    out = (out / math.sqrt(fft_len)).astype(np.float32)
    high = out.astype(ml_dtypes.bfloat16)
    low = (out - high.astype(np.float32)).astype(ml_dtypes.bfloat16)
    return np.concatenate([high, low], axis=1)


def first_step(x):
    c1, c2, c3 = (math.cos(math.pi * j / 8) for j in (1, 2, 3))
    a = [x[n] + x[n + 8] for n in range(8)]
    b = [x[n] - x[n + 8] for n in range(8)]
    d = [None] + [b[n] - b[8 - n] for n in (1, 2, 3)]
    s = [None] + [b[n] + b[8 - n] for n in (1, 2, 3)]
    u, v = b[0] + c2 * d[2], b[0] - c2 * d[2]
    p, q = c1 * d[1] + c3 * d[3], c3 * d[1] - c1 * d[3]
    g, h = b[4] + c2 * s[2], b[4] - c2 * s[2]
    m, n = c3 * s[1] + c1 * s[3], c1 * s[1] - c3 * s[3]
    e = [a[n_] + a[n_ + 4] for n_ in range(4)]
    f = [a[n_] - a[n_ + 4] for n_ in range(4)]
    w, z = c2 * (f[1] - f[3]), c2 * (f[1] + f[3])
    even, odd = e[0] + e[2], e[1] + e[3]
    return [
        (even + odd, even - odd),
        (u + p, g + m),
        (f[0] + w, f[2] + z),
        (v + q, n - h),
        (e[0] - e[2], e[1] - e[3]),
        (v - q, h + n),
        (f[0] - w, z - f[2]),
        (u - p, m - g),
    ]


def filter_outputs(plan, fft_len, keep, sources, taps_ref, base_ref, out_ref, start):
    rows = sources[0].shape[0]

    @pl.loop(0, RADIX)
    def _(col):
        base = pl.multiple_of(col * LANES, LANES)
        lanes = pl.ds(base, LANES)
        weights = [jnp.broadcast_to(taps_ref[pl.ds(j, 1), lanes], (rows, LANES)) for j in range(taps_ref.shape[0])]
        for block in range(0, len(plan), BLOCK):
            held = {}
            for out in range(block, min(block + BLOCK, len(plan))):
                at = pl.ds((start + out) * rows, rows)
                sums = {False: None if base_ref is None else base_ref[at, lanes], True: None}
                for j, src, frame, wiped in plan[out]:
                    if (src, frame) not in held:
                        lane = pl.multiple_of(frame * fft_len + base, LANES)
                        held[src, frame] = sources[src][:, pl.ds(lane, LANES)].astype(jnp.float32)
                    term = held[src, frame] * weights[j]
                    sums[wiped] = term if sums[wiped] is None else sums[wiped] + term
                total = sums[False]
                if sums[True] is not None:
                    wiped_sum = jnp.where(keep, sums[True], 0.0)
                    total = wiped_sum if total is None else total + wiped_sum
                out_ref[at, lanes] = total


def first_steps(filt, rows, first, count, high, low, offset, unroll=1):
    @pl.loop(0, count, unroll=unroll)
    def _(out):
        at = pl.ds(pl.multiple_of((out + first) * rows, rows), rows)
        to = pl.ds(pl.multiple_of(out * rows + offset, rows), rows)
        parts = first_step([filt[at, n * LANES : (n + 1) * LANES] for n in range(RADIX)])
        for pair, halves in enumerate(parts):
            for k, value in enumerate(halves):
                top = value.astype(jnp.bfloat16)
                high[pair, to, k * LANES : (k + 1) * LANES] = top
                low[pair, to, k * LANES : (k + 1) * LANES] = (value - top.astype(jnp.float32)).astype(jnp.bfloat16)


def second_steps(table, high, low, turned, ready, out_ref, half, sems):
    quarter = PLANE * Z_HIGH * Z_LOW
    per_dev = 4
    z_size = Z_HIGH * Z_LOW
    block = 2 * per_dev
    share = z_size * block
    cols = ready.shape[1]

    def product(left, right):
        return lax.dot_general(left, right, (((1,), (1,)), ((), ())), preferred_element_type=jnp.float32)

    def send(first_y, count, sem):
        copies = []
        for plane in range(PLANE):
            at = pl.ds((plane * Y_SIZE + first_y) * share, count * share)
            for lane in range(cols // LANES):
                ready[at, lane * LANES : (lane + 1) * LANES] = turned[lane, at].astype(jnp.bfloat16)
            copies.append(
                pltpu.make_async_copy(ready.at[at], out_ref.at[at, pl.ds(half * cols, cols)], sems.at[sem + plane])
            )
            copies[-1].start()
        return copies

    size = 2 * LANES
    copies = []
    for pair in range(RADIX // 2):
        table_high, table_low = table[pair, :size], table[pair, size:]
        both = product(table[pair], high[pair])
        result = (both[size:] + product(table_high, low[pair])) + both[:size]
        for slot in range(2):
            kappa = (pair, RADIX - pair)[slot] if pair else (0, RADIX // 2)[slot]
            for part in range(2):
                for plane in range(PLANE):
                    first = slot * LANES + part * quarter + plane * z_size
                    row = (plane * Y_SIZE + kappa // per_dev) * share + (kappa % per_dev) * 2 + part
                    for lane in range(cols // LANES):
                        turned[lane, pl.ds(row, z_size, stride=block), :] = result[
                            first : first + z_size, lane * LANES : (lane + 1) * LANES
                        ]
        if pair == 3:
            copies += send(0, 1, 0)
        if pair == 4:
            copies += send(3, 1, PLANE)
    return copies + send(1, 2, 2 * PLANE)


def middle_kernel(plan, own, fft_len, pairs_hbm, volts_hbm, taps_hbm, table_hbm, out_ref, more_high, more_low,
                  partial, taps, table, pairs_out, volts, filt, high, low, turned, ready, out_sems, sems):
    rows = volts.shape[0]
    keep = lax.axis_index("tm") != lax.axis_size("tm") - 1
    frames = volts.shape[1] // fft_len
    copies = [pltpu.make_async_copy(taps_hbm, taps, sems.at[0])]
    bounds = (0, 15, 21, 27, frames)
    for piece in range(4):
        part = pl.ds(bounds[piece] * fft_len, (bounds[piece + 1] - bounds[piece]) * fft_len)
        copies.append(pltpu.make_async_copy(volts_hbm.at[:, part], volts.at[:, part], sems.at[1 + piece]))
    copies.append(pltpu.make_async_copy(table_hbm, table, sems.at[5]))
    copies.append(pltpu.make_async_copy(pairs_hbm, pairs_out, sems.at[6]))
    for copy in copies:
        copy.start()
    copies[0].wait()
    done = 0
    for piece in range(4):
        copies[1 + piece].wait()
        upto = bounds[piece + 1] - (taps.shape[0] - 1)
        filter_outputs(plan[done:upto], fft_len, keep, [volts], taps, None, filt, done)
        done = upto
    first_steps(filt, rows, 0, HALF, high, low, 0)
    copies[5].wait()
    sent = second_steps(table, high, low, turned, ready, out_ref, 0, out_sems)
    filter_outputs(own, fft_len, keep, [volts], taps, None, partial, 0)
    first_steps(filt, rows, HALF, len(plan) - HALF, more_high, more_low, 0)
    for copy in [copies[6], *sent]:
        copy.wait()


def edge_kernel(plan, fft_len, taps, table, earlier, later, partial, more_high, more_low, _, out_ref,
                filt, high, low, turned, ready, out_sems, sems):
    rows = earlier.shape[0]
    copies = [
        pltpu.make_async_copy(more_high, high.at[:, pl.ds(0, more_high.shape[1])], sems.at[0]),
        pltpu.make_async_copy(more_low, low.at[:, pl.ds(0, more_low.shape[1])], sems.at[1]),
    ]
    for copy in copies:
        copy.start()
    filter_outputs(plan, fft_len, None, [earlier, later], taps, partial, filt, 0)
    first_steps(filt, rows, 0, len(plan), high, low, more_high.shape[1], len(plan))
    for copy in copies:
        copy.wait()
    for copy in second_steps(table, high, low, turned, ready, out_ref, 1, out_sems):
        copy.wait()


def spectra_scratch(rows, fft_len, outputs):
    cols = HALF * rows
    return [
        pltpu.VMEM((outputs * rows, fft_len), jnp.float32),
        pltpu.VMEM((RADIX // 2, cols, 2 * LANES), jnp.bfloat16),
        pltpu.VMEM((RADIX // 2, cols, 2 * LANES), jnp.bfloat16),
        pltpu.VMEM((cols // LANES, fft_len + 8, LANES), jnp.float32),
        pltpu.VMEM((fft_len, cols), jnp.bfloat16),
        pltpu.SemaphoreType.DMA((3 * PLANE,)),
    ]


def middle_call(plan, own, tile_pairs, volts, taps, table):
    rows, fft_len = volts.shape[0], taps.shape[1]
    cols = HALF * rows
    more = jax.ShapeDtypeStruct((RADIX // 2, (len(plan) - HALF) * rows, 2 * LANES), jnp.bfloat16)
    partial = jax.ShapeDtypeStruct((len(own) * rows, fft_len), jnp.float32)
    hbm = pl.BlockSpec(memory_space=pltpu.HBM)
    vmem = pl.BlockSpec(memory_space=pltpu.VMEM)
    smem = pl.BlockSpec(memory_space=pltpu.SMEM)
    return pl.pallas_call(
        functools.partial(middle_kernel, plan, own, fft_len),
        out_shape=(
            pltpu.HBM((fft_len, 2 * cols), jnp.bfloat16),
            *(pltpu.VMEM(x.shape, x.dtype) for x in (more, more, partial, taps, table)),
            pltpu.SMEM(tile_pairs.shape, tile_pairs.dtype),
        ),
        in_specs=[hbm, hbm, hbm, hbm],
        out_specs=(hbm, vmem, vmem, vmem, vmem, vmem, smem),
        scratch_shapes=[pltpu.VMEM(volts.shape, volts.dtype)]
        + spectra_scratch(rows, fft_len, len(plan))
        + [pltpu.SemaphoreType.DMA((7,))],
        compiler_params=pltpu.CompilerParams(vmem_limit_bytes=VMEM_LIMIT),
        cost_estimate=pl.CostEstimate(flops=10**9, bytes_accessed=8 * 2**20, transcendentals=0),
        name="middle",
    )(*(pltpu.with_memory_space_constraint(x, pltpu.HBM) for x in (tile_pairs, volts, taps, table)))


def edge_call(plan, taps, table, earlier, later, partial, more_high, more_low, spectra):
    rows, fft_len = earlier.shape[0], taps.shape[1]
    hbm = pl.BlockSpec(memory_space=pltpu.HBM)
    vmem = pl.BlockSpec(memory_space=pltpu.VMEM)
    anywhere = pl.BlockSpec(memory_space=pl.ANY)
    return pl.pallas_call(
        functools.partial(edge_kernel, plan, fft_len),
        out_shape=pltpu.HBM(spectra.shape, spectra.dtype),
        in_specs=[vmem, vmem, vmem, vmem, vmem, anywhere, anywhere, hbm],
        out_specs=hbm,
        scratch_shapes=spectra_scratch(rows, fft_len, len(plan)) + [pltpu.SemaphoreType.DMA((2,))],
        input_output_aliases={7: 0},
        compiler_params=pltpu.CompilerParams(vmem_limit_bytes=VMEM_LIMIT),
        cost_estimate=pl.CostEstimate(flops=10**9, bytes_accessed=8 * 2**20, transcendentals=0),
        name="edge",
    )(
        taps, table, earlier, later, partial, more_high, more_low, spectra,
    )


def ends_kernel(volts, last_ref, first_ref, sems):
    copies = []
    for ref, start in ((last_ref, volts.shape[1] - last_ref.shape[1]), (first_ref, 0)):
        for piece in range(0, ref.shape[1], ENDS_PIECE):
            size = min(ENDS_PIECE, ref.shape[1] - piece)
            copies.append(
                pltpu.make_async_copy(
                    volts.at[:, pl.ds(start + piece, size)], ref.at[:, pl.ds(piece, size)], sems.at[len(copies)]
                )
            )
    for copy in copies:
        copy.start()
    for copy in copies:
        copy.wait()


def ends_call(volts, last, first):
    vmem = pl.BlockSpec(memory_space=pltpu.VMEM)
    rows = volts.shape[0]
    return pl.pallas_call(
        ends_kernel,
        out_shape=(pltpu.VMEM((rows, last), volts.dtype), pltpu.VMEM((rows, first), volts.dtype)),
        in_specs=[pl.BlockSpec(memory_space=pltpu.HBM)],
        out_specs=(vmem, vmem),
        scratch_shapes=[pltpu.SemaphoreType.DMA((-(-last // ENDS_PIECE) - (-first // ENDS_PIECE),))],
        name="ends",
    )(pltpu.with_memory_space_constraint(volts, pltpu.HBM))


def gram_kernel(scale, pairs_ref, got_ref, out_ref, wide, both, tiles, sems):
    groups = wide.shape[0]
    per_src = 8
    times = Y_SIZE * Z_LOW
    inputs = LANES // 8
    pitch = 3 * per_src
    stations = Z_HIGH * PLANE * inputs

    copies = []
    for chan in range(out_ref.shape[1]):
        for stn in range(Z_HIGH * PLANE):
            if chan == 0 and stn < PLANE:
                for two in range(stn * times, (stn + 1) * times):
                    from_rows = pl.ds(two * 2 * per_src, 2 * per_src)
                    for group in range(groups):
                        wide[group, pl.ds(two * pitch, 2 * per_src)] = got_ref[
                            from_rows, group * LANES : (group + 1) * LANES
                        ].astype(jnp.float32)
            at = pl.ds(stn * inputs, inputs)
            turned_at = pl.ds(stations + stn * inputs, inputs)
            first = (stn % PLANE) * times * pitch + (stn // PLANE) * per_src + chan * 2
            parts = [
                [wide[group, pl.ds(first + part, times, stride=pitch), :] for group in range(groups)] for part in range(2)
            ]
            plain = jnp.concatenate(parts[0] + parts[1], 0).astype(jnp.bfloat16).T
            turned = jnp.concatenate([-v for v in parts[1]] + parts[0], 0).astype(jnp.bfloat16).T
            for t in range(LANES // inputs):
                cols = slice(t * LANES, (t + 1) * LANES)
                both[chan, at, cols] = plain[t * inputs : (t + 1) * inputs]
                both[chan, turned_at, cols] = turned[t * inputs : (t + 1) * inputs]
        sums = lax.dot_general(
            both[chan, :stations], both[chan], (((1,), (1,)), ((), ())), preferred_element_type=jnp.float32
        )
        for first in range(2):
            for second in range(2):
                for part in range(2):
                    col = part * stations + second * TILE
                    tiles[chan, first, second, part] = sums[first * TILE : (first + 1) * TILE, col : col + TILE] * scale
        for tile in range(pairs_ref.shape[1]):
            for part in range(2):
                copies.append(
                    pltpu.make_async_copy(
                        tiles.at[chan, pairs_ref[0, tile], pairs_ref[1, tile], part],
                        out_ref.at[part, chan, tile],
                        sems.at[len(copies)],
                    )
                )
                copies[-1].start()
    for copy in copies:
        copy.wait()


def gram_call(got, tile_pairs, chans, total_spectra):
    rows, lanes = got.shape
    stations = 2 * TILE
    depth = 8 * LANES
    tiles = tile_pairs.shape[1]
    return pl.pallas_call(
        functools.partial(gram_kernel, 1.0 / total_spectra),
        out_shape=jax.ShapeDtypeStruct((2, chans, tiles, TILE, TILE), jnp.float32),
        in_specs=[pl.BlockSpec(memory_space=pltpu.SMEM), pl.BlockSpec(memory_space=pltpu.VMEM)],
        out_specs=pl.BlockSpec(memory_space=pl.ANY),
        scratch_shapes=[
            pltpu.VMEM((lanes // LANES, rows // 2 * 3 + 24, LANES), jnp.float32),
            pltpu.VMEM((chans, 2 * stations, depth), jnp.bfloat16),
            pltpu.VMEM((chans, 2, 2, 2, TILE, TILE), jnp.float32),
            pltpu.SemaphoreType.DMA((2 * chans * tiles,)),
        ],
        compiler_params=pltpu.CompilerParams(vmem_limit_bytes=VMEM_LIMIT),
        name="grams",
    )(tile_pairs, got)


def plans(frames, tap_count):
    ahead = tap_count - 1 - BACK

    def taps(out):
        own, others = [], []
        for j in range(tap_count):
            frame = out - (tap_count - 1) + j
            if frame < 0:
                others.append((j, 0, frame + ahead, False))
            elif frame >= frames:
                others.append((j, 1, frame - frames, False))
            else:
                own.append((j, 0, frame, out >= frames))
        return own, others

    middle = [taps(out)[0] for out in range(tap_count - 1, frames)]
    edges = [taps(out) for out in [*range(BACK, tap_count - 1), *range(frames, frames + BACK)]]
    return middle, [own for own, _ in edges], [others for _, others in edges]


def shards(volts, taps, tile_pairs):
    tap_count, fft_len = taps.shape
    frames = volts.shape[1] // fft_len
    peers = lax.axis_size("tm")
    last, first = ends_call(volts, (tap_count - 1 - BACK) * fft_len, BACK * fft_len)
    earlier = lax.ppermute(last, "tm", [(i, i + 1) for i in range(peers - 1)])
    later = lax.ppermute(first, "tm", [(i, (i - 1) % peers) for i in range(peers)])
    table = jnp.asarray(second_step_table(fft_len))
    middle, own, others = plans(frames, tap_count)
    spectra, more_high, more_low, partial, taps, table, pairs = middle_call(middle, own, tile_pairs.T, volts, taps, table)
    spectra = edge_call(others, taps, table, earlier, later, partial, more_high, more_low, spectra)
    order = device_order()
    chans = fft_len // 2 // len(order)
    blocks = spectra.reshape(len(order), 2 * chans, spectra.shape[1])
    got = lax.all_to_all(
        blocks, ("stn", "tm"), split_axis=0, concat_axis=0, tiled=True, axis_index_groups=[order]
    )
    return gram_call(got.reshape(spectra.shape), pairs, chans, frames * peers)


def solution(mesh):
    return jax.shard_map(
        shards,
        mesh=mesh,
        in_specs=(P("stn", "tm"), P(), P()),
        out_specs=P(None, ("stn", "tm"), None, None, None),
        check_vma=False,
    )
```
